512 devices in a mesh: dp: 16 (over y, core), seq: 32 (over z, x).
Axes of the slice: x: 4, y: 8, z: 8, core: 2. Of those that a mesh axis runs over, the one named last changes fastest.
Arguments:
- queries: bfloat16 [16, 4096, 2048], P('dp', 'seq'), may hold values from -6 to 6
- keys: bfloat16 [16, 4096, 2048], P('dp', 'seq'), may hold values from -6 to 6
- values: bfloat16 [16, 4096, 2048], P('dp', 'seq'), may hold values from -6 to 6
- out_grad: bfloat16 [16, 4096, 2048], P('dp', 'seq'), may hold values from -21 to 21
- cluster_perm: int32 [16, 4096], P('dp'), may hold values from 0 to 4095, each once within a row
- tile_ids: int32 [16, 32, 8], P('dp'), may hold values from 0 to 31, as said below
- tile_counts: int32 [16, 32], P('dp'), may hold values from 1 to 8, 128 in all within a row
- hop_class: int32 [16, 32, 8], P('dp'), may hold values from 0 to 7
- hop_bias: float32 [8, 32], replicated, may hold values from -2 to 2
Outputs:
- attended: bfloat16 [16, 4096, 2048], P('dp', 'seq')
- query_grad: bfloat16 [16, 4096, 2048], P('dp', 'seq')
- key_grad: bfloat16 [16, 4096, 2048], P('dp', 'seq')
- value_grad: bfloat16 [16, 4096, 2048], P('dp', 'seq')
- bias_grad: float32 [8, 32], replicated
The draws below stay inside these ranges and needn't reach their ends.
Inputs may be any that keep to these rules, and one draw needn't show every extreme that they name: `tile_ids`: slot 0 of query tile t holds t; the 8 slots of a query tile name distinct tiles; slots at or past the tile's count are not used.
All inputs are finite; a program needn't handle non-finite values.
Results may differ from the reference program's by a relative error of at most 0.011.
Values may be sent and summed in bfloat16 or wider, within the bound.
A program may use at most 64 MiB of HBM per device.

```python
import math
import jax
import jax.numpy as jnp
import numpy as np
from jax import lax

HEADS = 32
HDIM = 64
TILE = 128
TP = 8
CLASSES = 8
GROUPS = 16
NODES = 4096
QT = 32


def draw_queries(key, part):
    key = jax.random.fold_in(key, 1)
    shape_all = (GROUPS, NODES, HEADS * HDIM)
    result = jnp.clip(jax.random.normal(key, shape_all, jnp.float32), -6.0, 6.0)
    return result.astype(jnp.bfloat16)


def draw_keys(key, part):
    key = jax.random.fold_in(key, 2)
    shape_all = (GROUPS, NODES, HEADS * HDIM)
    result = jnp.clip(jax.random.normal(key, shape_all, jnp.float32), -6.0, 6.0)
    return result.astype(jnp.bfloat16)


def draw_out_grad(key, part):
    key = jax.random.fold_in(key, 3)
    shape_all = (GROUPS, NODES, HEADS * HDIM)
    group_scale = 1.0 + 2.0 * jnp.arange(GROUPS).astype(jnp.float32) / max(GROUPS - 1, 1)
    result = jnp.clip(jax.random.normal(key, shape_all, jnp.float32), -6.0, 6.0)
    return (result * group_scale[:, None, None]).astype(jnp.bfloat16)


def draw_tile_ids(key, part):
    key = jax.random.fold_in(key, 4)
    ranks = jax.random.randint(key, (GROUPS, QT, QT - 1), 0, 1 << 20) * QT + jnp.arange(QT - 1)[None, None, :]
    order_all = jnp.argsort(ranks, axis=-1, stable=True).astype(jnp.int32)
    offsets = order_all[:, :, :TP - 1] + 1
    tile_index = jnp.arange(QT, dtype=jnp.int32)[None, :, None]
    others = (tile_index + offsets) % QT
    own = jnp.broadcast_to(tile_index, (GROUPS, QT, 1))
    return jnp.concatenate([own, others], axis=-1).astype(jnp.int32)


def set_ends(entries, stream_key, smallest, top_value):
    dims = entries.shape
    place = [jax.random.randint(jax.random.fold_in(stream_key, axis), (), 0, dims[axis]) for axis in range(len(dims))]
    entries = entries.at[tuple(place)].set(smallest)
    longest = dims.index(max(dims))
    place[longest] = (place[longest] + 1) % dims[longest]
    return entries.at[tuple(place)].set(top_value)


def levels(rng, extent, pieces, low, high):
    loudness = 1.0
    for position, shards_of in pieces:
        draws = jax.random.uniform(jax.random.fold_in(jax.random.fold_in(rng, 6), position), (shards_of,), jnp.float32, low / len(pieces), high / len(pieces))
        loudness = loudness * jnp.repeat(jnp.exp(draws), extent[position] // shards_of).reshape((-1,) + (1,) * (len(extent) - 1 - position))
    return loudness


def split_up(number_of, total, reach, skew):
    loads = [(1 << 20) // math.isqrt(rank ** skew) + 1 for rank in range(2, number_of + 1)]
    rest, counts = total - reach - (number_of - 1), [1] * (number_of - 1)
    while rest > 0:
        movable = [i for i in range(number_of - 1) if counts[i] < reach]
        pool, budget = sum([loads[i] for i in movable]), rest
        for i in movable:
            more = min(reach - counts[i], max(1, budget * loads[i] // pool), rest)
            counts[i] = counts[i] + more
            rest = rest - more
    return np.array([reach] + counts)


def uneven(stream_key, amount, total, limit, slope):
    if amount == 2:
        one = jax.random.randint(stream_key, (), max(1, total - limit), min(limit, total - 1) + 1)
        return jnp.stack([one, total - one])
    tallies = jnp.asarray(split_up(amount, total, limit, slope), jnp.int32)
    pairs = (amount - 1) // 2
    giver, receiver = tallies[1:1 + 2 * pairs:2], tallies[2:2 + 2 * pairs:2]
    room = jnp.minimum(giver - 1, limit - receiver)
    moved = jax.random.randint(jax.random.fold_in(stream_key, 1), (pairs,), 0, 1 << 20) % (room + 1)
    tallies = tallies.at[1:1 + 2 * pairs:2].set(giver - moved).at[2:2 + 2 * pairs:2].set(receiver + moved)
    return tallies[jax.random.permutation(jax.random.fold_in(stream_key, 2), amount)]


def scatter_about(rng, dims, spread, bound, cuts=(), kind=jnp.bfloat16):
    factor_of = levels(rng, dims, cuts, -0.22, 0.18) if cuts else 1.0
    entries = jax.random.normal(rng, dims, jnp.float32) * spread * factor_of
    return jnp.minimum(jnp.maximum(entries, -bound), bound).astype(kind)


def setup_inputs(seed: int = 0) -> dict:
    splits = jax.random.split(jax.random.key(seed), 10)
    return {
        "queries": draw_queries(jax.random.fold_in(splits[9], 71), 0),
        "keys": draw_keys(jax.random.fold_in(splits[9], 71), 0),
        "values": scatter_about(splits[2], (GROUPS, NODES, HEADS * HDIM), 1.0, 6.0, ((0, 16), (1, 32))),
        "out_grad": draw_out_grad(jax.random.fold_in(splits[9], 71), 0),
        "cluster_perm": jax.vmap(lambda own: jax.random.permutation(own, NODES))(jax.random.split(splits[4], GROUPS)).reshape((GROUPS, NODES)).astype(jnp.int32),
        "tile_ids": draw_tile_ids(jax.random.fold_in(splits[9], 71), 0),
        "tile_counts": jax.vmap(lambda own: uneven(own, QT, QT * TP // 2, TP, 2))(jax.random.split(splits[6], GROUPS)).reshape((GROUPS, QT)).astype(jnp.int32),
        "hop_class": set_ends(jax.random.randint(splits[7], (GROUPS, QT, TP), 0, CLASSES), jax.random.fold_in(splits[7], 1), 0, CLASSES - 1).astype(jnp.int32),
        "hop_bias": jnp.clip(jax.random.uniform(splits[8], (CLASSES, HEADS), jnp.float32, -2.0, 2.0), -2.0, 2.0),
    }


exact_mode = lax.Precision.HIGHEST


def tile_pass(query_heads, key_heads, value_heads, grad_heads, tile_list, tile_count, class_list, bias_cols):
    node_total, local_heads, head_width = query_heads.shape
    tile_total = node_total // TILE
    slot_total = tile_list.shape[-1]
    classes = bias_cols.shape[0]
    steps_total = tile_total // 4
    key_tiles = key_heads.reshape(tile_total, TILE, local_heads, head_width)
    value_tiles = value_heads.reshape(tile_total, TILE, local_heads, head_width)

    def blocked(tensor):
        return tensor.reshape((steps_total, 4) + tensor.shape[1:])

    inputs = (blocked(query_heads.reshape(tile_total, TILE, local_heads, head_width)),
              blocked(grad_heads.reshape(tile_total, TILE, local_heads, head_width)),
              blocked(tile_list), blocked(tile_count), blocked(class_list))

    def advance(totals, inputs_now):
        query_now, grad_now, list_now, count_now, class_now = inputs_now
        query_wide = query_now.astype(jnp.float32)
        grad_wide = grad_now.astype(jnp.float32)
        key_now = key_tiles[list_now].astype(jnp.float32)
        value_now = value_tiles[list_now].astype(jnp.float32)
        class_hot = (class_now[..., None] == jnp.arange(classes)[None, None, :]).astype(jnp.float32)
        bias_now = jnp.einsum("qsc,ch->qhs", class_hot, bias_cols, precision=exact_mode)
        usable = jnp.arange(slot_total)[None, :] < count_now[:, None]
        scores = jnp.einsum("qahe,qsbhe->qhasb", query_wide, key_now) * 0.125 + bias_now[:, :, None, :, None]
        scores = jnp.where(usable[:, None, None, :, None], scores, -1e30)
        row_peak = jnp.max(scores, axis=(3, 4), keepdims=True)
        powers = jnp.exp(scores - row_peak)
        weights = powers / jnp.sum(powers, axis=(3, 4), keepdims=True)
        weights_low = weights.astype(jnp.bfloat16)
        weights_back = weights_low.astype(jnp.float32)
        attended = jnp.einsum("qhasb,qsbhe->qahe", weights_back, value_now).astype(jnp.bfloat16)
        prob_grad = jnp.einsum("qahe,qsbhe->qhasb", grad_wide, value_now)
        row_dot = jnp.sum(weights * prob_grad, axis=(3, 4), keepdims=True)
        score_grad = weights * (prob_grad - row_dot)
        slot_sums = jnp.sum(score_grad, axis=(2, 4))
        score_low = score_grad.astype(jnp.bfloat16).astype(jnp.float32)
        query_grad = (jnp.einsum("qhasb,qsbhe->qahe", score_low, key_now) * 0.125).astype(jnp.bfloat16)
        key_part = jnp.einsum("qhasb,qahe->qsbhe", score_low, query_wide) * 0.125
        value_part = jnp.einsum("qhasb,qahe->qsbhe", weights_back, grad_wide)
        placing = (list_now[..., None] == jnp.arange(tile_total)[None, None, :]).astype(jnp.float32)
        key_total = totals[0] + jnp.einsum("qst,qsbhe->tbhe", placing, key_part, precision=exact_mode)
        value_total = totals[1] + jnp.einsum("qst,qsbhe->tbhe", placing, value_part, precision=exact_mode)
        bias_total = totals[2] + jnp.einsum("qsc,qhs->ch", class_hot, slot_sums, precision=exact_mode)
        return (key_total, value_total, bias_total), (attended, query_grad)

    start = (jnp.zeros((tile_total, TILE, local_heads, head_width), jnp.float32),
             jnp.zeros((tile_total, TILE, local_heads, head_width), jnp.float32),
             jnp.zeros((classes, local_heads), jnp.float32))
    totals, stacked = lax.scan(advance, start, inputs)
    shape_back = (node_total, local_heads, head_width)
    return (stacked[0].reshape(shape_back), stacked[1].reshape(shape_back),
            totals[0].astype(jnp.bfloat16).reshape(shape_back),
            totals[1].astype(jnp.bfloat16).reshape(shape_back), totals[2])


def reference(queries, keys, values, out_grad, cluster_perm, tile_ids, tile_counts, hop_class, hop_bias):
    def one_group(group_inputs):
        query_group, key_group, value_group, grad_group, node_order, tile_list, tile_count, class_list = group_inputs

        def to_heads(tensor):
            return tensor.reshape(NODES, HEADS, HDIM)[node_order]

        results = tile_pass(to_heads(query_group), to_heads(key_group), to_heads(value_group),
                            to_heads(grad_group), tile_list, tile_count, class_list, hop_bias)
        inverse = jnp.argsort(node_order)

        def restore(tensor):
            return tensor[inverse].reshape(NODES, HEADS * HDIM)

        return (restore(results[0]), restore(results[1]), restore(results[2]),
                restore(results[3]), results[4])

    results = lax.map(one_group, (queries, keys, values, out_grad, cluster_perm, tile_ids, tile_counts, hop_class))
    return results[0], results[1], results[2], results[3], jnp.sum(results[4], axis=0)
```

```python
import functools
import math

import jax
import jax.numpy as jnp
from jax import lax
from jax.experimental import pallas as pl
from jax.experimental.pallas import tpu as pltpu
from jax.sharding import PartitionSpec as P

MESH = pl.DeviceIdType.MESH
TILE = 128
LOG2E = math.log2(math.e)
NT_DIMS = (((1,), (1,)), ((), ()))


def lanes_low(shape):
    return lax.broadcasted_iota(jnp.int32, shape, len(shape) - 1) < 64


def greet(me, count):
    dp = lax.axis_index("dp")
    barrier = pltpu.get_barrier_semaphore()

    @pl.loop(1, count)
    def _(step):
        other = lax.rem(me + step, count)
        pl.semaphore_signal(barrier, inc=1, device_id=(dp, other), device_id_type=MESH)

    return barrier


def remote(src, dst, send_sem, recv_sem, other):
    return pltpu.make_async_remote_copy(
        src_ref=src,
        dst_ref=dst,
        send_sem=send_sem,
        recv_sem=recv_sem,
        device_id=(lax.axis_index("dp"), other),
        device_id_type=MESH,
    )


def rolled(block):
    return pltpu.roll(block.astype(jnp.float32), 64, 1).astype(jnp.bfloat16)


def gather_rows(source, rows_out, base, index_of):
    for r in range(TILE):
        rows_out[pl.ds(r, 1), :] = source[pl.ds(index_of(base, r), 1), :]


def inbound_kernel(
    count,
    q_ref,
    k_ref,
    v_ref,
    g_ref,
    perm_ref,
    perm_row_ref,
    ids_ref,
    counts_ref,
    class_ref,
    kv_ref,
    kvt_ref,
    qg_ref,
    inverse_ref,
    pairs_ref,
    send_kv,
    send_qg,
    recv_kv,
    wide,
    rows,
    send_sem,
    recv_sem,
):
    me = lax.axis_index("seq")
    barrier = greet(me, count)
    low = lanes_low((TILE, TILE))

    def pack(first_ref, second_ref, out):
        @pl.loop(0, count // 2)
        def _(pair):
            columns = pl.ds(pl.multiple_of(pair * TILE, TILE), TILE)
            first, second = first_ref[:, columns], second_ref[:, columns]
            out[2 * pair] = jnp.where(low, first, rolled(second))
            out[2 * pair + 1] = jnp.where(low, rolled(first), second)

    def send_all(out, landing, which):
        @pl.loop(1, count)
        def _(step):
            other = lax.rem(me + step, count)
            remote(
                out.at[other], landing.at[me], send_sem.at[which], recv_sem.at[which], other
            ).start()

        landing[me] = out[me]

    def wait_all(out, landing, which, receive):
        many = remote(
            out.at[pl.ds(0, count - 1)],
            landing.at[pl.ds(0, count - 1)],
            send_sem.at[which],
            recv_sem.at[which],
            lax.rem(me + 1, count),
        )
        if receive:
            many.wait_recv()
        else:
            many.wait_send()

    pack(k_ref, v_ref, send_kv)
    pl.semaphore_wait(barrier, count - 1)
    send_all(send_kv, recv_kv, 0)
    pack(q_ref, g_ref, send_qg)
    send_all(send_qg, qg_ref, 1)

    def list_pair(p, state):
        t, s = state
        pairs_ref[0, p] = t
        pairs_ref[1, p] = ids_ref[0, t, s]
        pairs_ref[2, p] = class_ref[0, t, s]
        more = s + 1 < counts_ref[0, t]
        following = jnp.minimum(t + 1, counts_ref.shape[1] - 1)
        return jnp.where(more, t, following), jnp.where(more, s + 1, 0)

    lax.fori_loop(0, TILE, list_pair, (jnp.int32(0), jnp.int32(0)))

    high_total = jnp.zeros((64, 64), jnp.float32)
    low_total = jnp.zeros((64, 64), jnp.float32)
    width = 1024
    nodes = perm_row_ref.shape[1]
    for start in range(0, nodes, width):
        node = perm_row_ref[:, pl.ds(start, width)]
        digit = lax.broadcasted_iota(jnp.int32, (64, width), 0)
        position = lax.broadcasted_iota(jnp.int32, (64, width), 1) + start
        at_high = lax.shift_right_logical(node, 6) == digit
        at_low = jnp.where((node & 63) == digit, 1.0, 0.0).astype(jnp.bfloat16)
        high_value = lax.shift_right_logical(position, 6).astype(jnp.float32)
        low_value = (position & 63).astype(jnp.float32)
        high_rows = jnp.where(at_high, high_value, 0.0).astype(jnp.bfloat16)
        low_rows = jnp.where(at_high, low_value, 0.0).astype(jnp.bfloat16)
        high_total += lax.dot_general(high_rows, at_low, NT_DIMS, preferred_element_type=jnp.float32)
        low_total += lax.dot_general(low_rows, at_low, NT_DIMS, preferred_element_type=jnp.float32)
    inverse_ref[...] = (high_total * 64.0 + low_total).astype(jnp.int32)

    wait_all(send_kv, recv_kv, 0, True)

    @pl.loop(0, count)
    def _(block):
        wide[pl.ds(pl.multiple_of(block * TILE, TILE), TILE), :] = recv_kv[block].astype(jnp.float32)

    @pl.loop(0, count)
    def _(tile):
        gather_rows(wide, rows, tile * TILE, lambda base, r: perm_ref[0, base + r])
        block = rows[...]
        kv_ref[tile] = block.astype(jnp.bfloat16)
        kvt_ref[tile] = block.T.astype(jnp.bfloat16)

    wait_all(send_qg, qg_ref, 1, True)
    wait_all(send_kv, recv_kv, 0, False)
    wait_all(send_qg, qg_ref, 1, False)


def attention_kernel(
    unroll,
    kv_ref,
    kvt_ref,
    qg_ref,
    perm_ref,
    pairs_ref,
    bias_ref,
    oq_ref,
    dkv_ref,
    bias_out_ref,
    wide,
    rows,
    weight,
    scores,
    grads,
    peak,
    total,
    dots,
    dkv_acc,
    oq_acc,
    bias_acc,
):
    head = lax.axis_index("seq")
    tiles = kv_ref.shape[0]
    low = lanes_low((TILE, TILE))

    @pl.loop(0, tiles)
    def _(block):
        wide[pl.ds(pl.multiple_of(block * TILE, TILE), TILE), :] = qg_ref[block].astype(jnp.float32)

    @pl.loop(0, tiles)
    def _(tile):
        gather_rows(wide, rows, tile * TILE, lambda base, r: perm_ref[0, base + r])
        block = rows[...]
        weight[tile, pl.ds(0, TILE), :] = jnp.where(low, block * 0.125, 0.0).astype(jnp.bfloat16)
        weight[tile, pl.ds(TILE, TILE), :] = jnp.where(low, 0.0, block).astype(jnp.bfloat16)

    peak[...] = jnp.full(peak.shape, -jnp.inf, jnp.float32)
    total[...] = jnp.zeros(total.shape, jnp.float32)
    dots[...] = jnp.zeros(dots.shape, jnp.float32)
    dkv_acc[...] = jnp.zeros(dkv_acc.shape, jnp.float32)
    oq_acc[...] = jnp.zeros(oq_acc.shape, jnp.float32)
    bias_acc[...] = jnp.zeros(bias_acc.shape, jnp.float32)

    def folded(block):
        return block.reshape(TILE // 8, 8, TILE)

    @pl.loop(0, TILE // unroll)
    def _(step):
        for u in range(unroll):
            p = step * unroll + u
            t, j = pairs_ref[0, p], pairs_ref[1, p]
            bias = bias_ref[pairs_ref[2, p], head] * LOG2E
            both = lax.dot_general(kv_ref[j], weight[t], NT_DIMS, preferred_element_type=jnp.float32)
            score = both[:, :TILE] * LOG2E + bias
            scores[p] = score
            grads[p] = both[:, TILE:]
            peak[t] = jnp.maximum(peak[t], jnp.max(folded(score), axis=0))

    peak[...] = jnp.broadcast_to(jnp.max(peak[...], axis=1, keepdims=True), peak.shape)

    @pl.loop(0, TILE // unroll)
    def _(step):
        for u in range(unroll):
            p = step * unroll + u
            t = pairs_ref[0, p]
            power = jnp.exp2(folded(scores[p]) - peak[t][None])
            scores[p] = power.reshape(TILE, TILE)
            total[t] = total[t] + jnp.sum(power, axis=0)
            dots[t] = dots[t] + jnp.sum(power * folded(grads[p]), axis=0)

    scale = 1.0 / jnp.sum(total[...], axis=1, keepdims=True)
    delta = jnp.sum(dots[...], axis=1, keepdims=True) * scale
    total[...] = jnp.broadcast_to(scale, total.shape)
    dots[...] = jnp.broadcast_to(delta, dots.shape)

    @pl.loop(0, TILE // unroll)
    def _(step):
        for u in range(unroll):
            p = step * unroll + u
            t, j, c = pairs_ref[0, p], pairs_ref[1, p], pairs_ref[2, p]
            prob = folded(scores[p]) * total[t][None]
            score_grad = prob * (folded(grads[p]) - dots[t][None])
            bias_acc[c] = bias_acc[c] + jnp.sum(score_grad, axis=0)
            prob_low = prob.reshape(TILE, TILE).astype(jnp.bfloat16)
            grad_low = score_grad.reshape(TILE, TILE).astype(jnp.bfloat16)
            dkv_acc[j] = dkv_acc[j] + jnp.dot(
                jnp.concatenate([grad_low, prob_low], axis=1),
                weight[t],
                preferred_element_type=jnp.float32,
            )
            kvt = kvt_ref[j]
            oq_acc[t, pl.ds(0, 64), :] = oq_acc[t, pl.ds(0, 64), :] + jnp.dot(
                kvt[:64], grad_low, preferred_element_type=jnp.float32
            )
            oq_acc[t, pl.ds(64, 64), :] = oq_acc[t, pl.ds(64, 64), :] + jnp.dot(
                kvt[64:], prob_low, preferred_element_type=jnp.float32
            )

    @pl.loop(0, tiles)
    def _(tile):
        block = oq_acc[tile].T
        oq_ref[tile] = jnp.where(low, block * 0.125, block)
        dkv_ref[tile] = dkv_acc[tile]

    class_sums = jnp.sum(jnp.sum(bias_acc[...], axis=1), axis=1, keepdims=True)
    column = lax.broadcasted_iota(jnp.int32, bias_out_ref.shape, 1)
    bias_out_ref[...] = jnp.where(column == head, class_sums, 0.0)


def outbound_kernel(
    count,
    oq_ref,
    dkv_ref,
    inverse_ref,
    bias_ref,
    o_ref,
    dq_ref,
    dk_ref,
    dv_ref,
    bias_out_ref,
    send_oq,
    send_dkv,
    recv_oq,
    recv_dkv,
    rows,
    bias_groups,
    bias_sum,
    bias_heads,
    send_sem,
    recv_sem,
):
    me = lax.axis_index("seq")
    group, groups = lax.axis_index("dp"), bias_groups.shape[0]
    barrier = greet(me, count)

    @pl.loop(1, groups)
    def _(step):
        other = lax.rem(group + step, groups)
        pl.semaphore_signal(barrier, inc=1, device_id=(other, me), device_id_type=MESH)

    low = lanes_low((TILE, TILE))
    pl.semaphore_wait(barrier, count + groups - 2)

    def bias_to_group(step):
        other = lax.rem(group + step, groups)
        return pltpu.make_async_remote_copy(
            src_ref=bias_ref,
            dst_ref=bias_groups.at[group],
            send_sem=send_sem.at[2],
            recv_sem=recv_sem.at[2],
            device_id=(other, me),
            device_id_type=MESH,
        )

    @pl.loop(1, groups)
    def _(step):
        bias_to_group(step).start()

    bias_groups[group] = bias_ref[...]

    def send_all(source, out, landing, which):
        def fill(other):
            gather_rows(
                source,
                rows,
                other,
                lambda base, r: inverse_ref[2 * base + r // 64, r % 64],
            )
            return rows[...].astype(jnp.bfloat16)

        @pl.loop(1, count)
        def _(step):
            other = lax.rem(me + step, count)
            out[other] = fill(other)
            remote(
                out.at[other], landing.at[me], send_sem.at[which], recv_sem.at[which], other
            ).start()

        landing[me] = fill(me)

    def wait_all(out, landing, which, receive, parties=count):
        many = remote(
            out.at[pl.ds(0, parties - 1)],
            landing.at[pl.ds(0, parties - 1)],
            send_sem.at[which],
            recv_sem.at[which],
            lax.rem(me + 1, count),
        )
        if receive:
            many.wait_recv()
        else:
            many.wait_send()

    def unpack(landing, first_ref, second_ref):
        @pl.loop(0, count // 2)
        def _(pair):
            columns = pl.ds(pl.multiple_of(pair * TILE, TILE), TILE)
            even, odd = landing[2 * pair], landing[2 * pair + 1]
            first_ref[:, columns] = jnp.where(low, even, rolled(odd))
            second_ref[:, columns] = jnp.where(low, rolled(even), odd)

    send_all(oq_ref, send_oq, recv_oq, 0)
    wait_all(bias_groups, bias_groups, 2, True, groups)
    bias_sum[...] = jnp.sum(bias_groups[...], axis=0)

    @pl.loop(1, count)
    def _(step):
        other = lax.rem(me + step, count)
        remote(bias_sum, bias_heads.at[me], send_sem.at[3], recv_sem.at[3], other).start()

    bias_heads[me] = bias_sum[...]
    send_all(dkv_ref, send_dkv, recv_dkv, 1)
    wait_all(bias_heads, bias_heads, 3, True)
    bias_out_ref[...] = jnp.sum(bias_heads[...], axis=0)[:, : bias_out_ref.shape[1]]
    wait_all(send_oq, recv_oq, 0, True)
    unpack(recv_oq, dq_ref, o_ref)
    wait_all(send_dkv, recv_dkv, 1, True)
    unpack(recv_dkv, dk_ref, dv_ref)
    wait_all(send_oq, recv_oq, 0, False)
    wait_all(send_dkv, recv_dkv, 1, False)
    wait_all(bias_groups, bias_groups, 2, False, groups)
    wait_all(bias_heads, bias_heads, 3, False)


def local(
    queries, keys, values, out_grad, cluster_perm, tile_ids, tile_counts, hop_class, hop_bias
):
    count = lax.axis_size("seq")
    nodes = cluster_perm.shape[1]
    tiles = nodes // TILE
    columns = queries.shape[2]
    classes, heads = hop_bias.shape
    vmem = pl.BlockSpec(memory_space=pltpu.VMEM)
    smem = pl.BlockSpec(memory_space=pltpu.SMEM)
    bf16, f32 = jnp.bfloat16, jnp.float32
    blocks = (count, TILE, TILE)

    kv, kvt, qg, inverse, pairs = pl.pallas_call(
        functools.partial(inbound_kernel, count),
        out_shape=(
            jax.ShapeDtypeStruct(blocks, bf16),
            jax.ShapeDtypeStruct(blocks, bf16),
            jax.ShapeDtypeStruct(blocks, bf16),
            jax.ShapeDtypeStruct((64, 64), jnp.int32),
            jax.ShapeDtypeStruct((3, TILE), jnp.int32),
        ),
        in_specs=[vmem] * 4 + [smem, vmem] + [smem] * 3,
        out_specs=(vmem, vmem, vmem, vmem, smem),
        scratch_shapes=[
            pltpu.VMEM(blocks, bf16),
            pltpu.VMEM(blocks, bf16),
            pltpu.VMEM(blocks, bf16),
            pltpu.VMEM((nodes, TILE), f32),
            pltpu.VMEM((TILE, TILE), f32),
            pltpu.SemaphoreType.DMA((2,)),
            pltpu.SemaphoreType.DMA((2,)),
        ],
        compiler_params=pltpu.CompilerParams(
            collective_id=0, has_side_effects=True, vmem_limit_bytes=32 << 20
        ),
        name="inbound",
    )(
        queries[0],
        keys[0],
        values[0],
        out_grad[0],
        cluster_perm,
        cluster_perm,
        tile_ids,
        tile_counts,
        hop_class,
    )

    oq, dkv, bias_part = pl.pallas_call(
        functools.partial(attention_kernel, 4),
        out_shape=(
            jax.ShapeDtypeStruct((tiles, TILE, TILE), f32),
            jax.ShapeDtypeStruct((tiles, TILE, TILE), f32),
            jax.ShapeDtypeStruct((classes, TILE), f32),
        ),
        in_specs=[vmem] * 3 + [smem] * 3,
        out_specs=(vmem,) * 3,
        scratch_shapes=[
            pltpu.VMEM((nodes, TILE), f32),
            pltpu.VMEM((TILE, TILE), f32),
            pltpu.VMEM((tiles, 2 * TILE, TILE), bf16),
            pltpu.VMEM((TILE, TILE, TILE), f32),
            pltpu.VMEM((TILE, TILE, TILE), f32),
            pltpu.VMEM((tiles, 8, TILE), f32),
            pltpu.VMEM((tiles, 8, TILE), f32),
            pltpu.VMEM((tiles, 8, TILE), f32),
            pltpu.VMEM((tiles, TILE, TILE), f32),
            pltpu.VMEM((tiles, TILE, TILE), f32),
            pltpu.VMEM((classes, 8, TILE), f32),
        ],
        compiler_params=pltpu.CompilerParams(vmem_limit_bytes=48 << 20),
        name="attention",
    )(kv, kvt, qg, cluster_perm, pairs, hop_bias)

    one_output = jax.ShapeDtypeStruct((TILE, columns), bf16)
    attended, query_grad, key_grad, value_grad, bias_grad = pl.pallas_call(
        functools.partial(outbound_kernel, count),
        out_shape=(one_output,) * 4 + (jax.ShapeDtypeStruct((classes, heads), f32),),
        in_specs=[vmem, vmem, smem, vmem],
        out_specs=(vmem,) * 5,
        scratch_shapes=[
            pltpu.VMEM(blocks, bf16),
            pltpu.VMEM(blocks, bf16),
            pltpu.VMEM(blocks, bf16),
            pltpu.VMEM(blocks, bf16),
            pltpu.VMEM((TILE, TILE), f32),
            pltpu.VMEM((lax.axis_size("dp"), classes, TILE), f32),
            pltpu.VMEM((classes, TILE), f32),
            pltpu.VMEM((count, classes, TILE), f32),
            pltpu.SemaphoreType.DMA((4,)),
            pltpu.SemaphoreType.DMA((4,)),
        ],
        compiler_params=pltpu.CompilerParams(
            collective_id=1, has_side_effects=True, vmem_limit_bytes=32 << 20
        ),
        name="outbound",
    )(oq.reshape(nodes, TILE), dkv.reshape(nodes, TILE), inverse, bias_part)

    return attended[None], query_grad[None], key_grad[None], value_grad[None], bias_grad


def solution(mesh):
    wide = P("dp", "seq", None)
    return jax.shard_map(
        local,
        mesh=mesh,
        in_specs=(
            wide,
            wide,
            wide,
            wide,
            P("dp", None),
            P("dp", None, None),
            P("dp", None),
            P("dp", None, None),
            P(),
        ),
        out_specs=(wide, wide, wide, wide, P()),
        check_vma=False,
    )
```

```python
import functools
import math

import jax
import jax.numpy as jnp
from jax import lax
from jax.experimental import pallas as pl
from jax.experimental.pallas import tpu as pltpu
from jax.sharding import PartitionSpec as P

MESH = pl.DeviceIdType.MESH
TILE = 128
LOG2E = math.log2(math.e)
NT_DIMS = (((1,), (1,)), ((), ()))
BF16, F32 = jnp.bfloat16, jnp.float32
UNROLL = 32
ABREAST = 4

T_OF, J_OF, P_OF, TQ_OF, JQ_OF, T_LAST, J_LAST = range(7)


def iota(shape, axis):
    return lax.broadcasted_iota(jnp.int32, shape, axis)


def lanes_low():
    return iota((TILE, TILE), 1) < 64


def rolled(block):
    return pltpu.roll(block.astype(F32), 64, 1).astype(BF16)


def folded(block):
    return block.reshape(TILE // 8, 8, TILE)


def gather_rows(source, rows_out, index_of):
    for r in range(TILE):
        rows_out[pl.ds(r, 1), :] = source[pl.ds(index_of(r), 1), :]


def unrolled(count, factor, body):
    def turn(step, carry):
        for u in range(factor):
            body(step * factor + u)
        return carry

    lax.fori_loop(0, count // factor, turn, jnp.int32(0))


def write_lists(head, ids_ref, counts_ref, class_ref, bias_ref, list_ref, pair_bias_ref, hot_ref):
    slots, tiles = ids_ref.shape[1], ids_ref.shape[2]
    flat = tiles * slots
    lane_slot = iota((tiles, flat), 1) % slots
    own = iota((tiles, flat), 1) // slots == iota((tiles, flat), 0)

    diagonal = iota((tiles, tiles), 0) == iota((tiles, tiles), 1)

    def upright(row):
        return jnp.sum(jnp.where(diagonal, row, 0.0), axis=1, keepdims=True)

    def flat_row(table):
        spread = jnp.zeros((tiles, flat), F32)
        for s in range(slots):
            spread = jnp.where(lane_slot == s, upright(table[s : s + 1, :]), spread)
        return jnp.sum(jnp.where(own, spread, 0.0), axis=0, keepdims=True)

    def column(row):
        return jnp.broadcast_to(row, (TILE, flat)).T

    counts = upright(counts_ref[...].astype(F32))
    used = jnp.sum(
        jnp.where(own & (lane_slot.astype(F32) < counts), 1.0, 0.0), axis=0, keepdims=True
    )
    tile_row = flat_row(ids_ref[0].astype(F32))
    class_row = flat_row(class_ref[0].astype(F32))
    used_col, tile_col, class_col = column(used), column(tile_row), column(class_row)
    place = iota((flat, TILE), 0)
    place_wide = place.astype(F32)
    query_col = (place // slots).astype(F32)
    lane = iota((flat, TILE), 1).astype(F32)

    def ranks(key_col, key_row):
        parts = []
        for start in range(0, flat, TILE):
            before = (used_col > 0.5) & (key_col < key_row[:, start : start + TILE])
            parts.append(jnp.sum(jnp.where(before, 1.0, 0.0), axis=0, keepdims=True))
        return column(jnp.concatenate(parts, axis=1))

    place_row = iota((1, flat), 1).astype(F32)
    by_query = ranks(place_wide, place_row)
    by_key = ranks(tile_col * flat + place_wide, tile_row * flat + place_row)

    def pick(rank, values):
        return jnp.sum(
            jnp.where((rank == lane) & (used_col > 0.5), values, 0.0), axis=0, keepdims=True
        )

    def last(values):
        reached = (used_col > 0.5) & (values <= lane)
        return jnp.sum(jnp.where(reached, 1.0, 0.0), axis=0, keepdims=True) - 1.0

    class_of = pick(by_query, class_col)
    rows = (
        pick(by_query, query_col),
        pick(by_query, tile_col),
        pick(by_key, by_query),
        pick(by_key, query_col),
        pick(by_key, tile_col),
        last(query_col),
        last(tile_col),
    )
    table = jnp.concatenate(rows + (jnp.zeros((8 - len(rows), TILE), F32),), axis=0)
    list_ref[...] = jnp.clip(table.astype(jnp.int32), 0, TILE - 1)

    classes, heads = bias_ref.shape
    hot = jnp.where(iota((classes, TILE), 0).astype(F32) == class_of, 1.0, 0.0)
    hot_ref[...] = hot
    own_bias = jnp.sum(
        jnp.where(iota((classes, heads), 1) == head, bias_ref[...], 0.0), axis=1, keepdims=True
    )
    pair_bias = jnp.sum(hot * own_bias, axis=0, keepdims=True) * LOG2E
    pair_bias_ref[...] = jnp.broadcast_to(pair_bias, pair_bias_ref.shape)


def write_inverse(perm_ref, inverse_ref):
    high_total = jnp.zeros((64, 64), F32)
    low_total = jnp.zeros((64, 64), F32)
    width = 1024
    for start in range(0, perm_ref.shape[1], width):
        node = perm_ref[:, pl.ds(start, width)]
        digit = iota((64, width), 0)
        position = iota((64, width), 1) + start
        at_high = lax.shift_right_logical(node, 6) == digit
        at_low = jnp.where((node & 63) == digit, 1.0, 0.0).astype(BF16)
        high_value = lax.shift_right_logical(position, 6).astype(F32)
        low_value = (position & 63).astype(F32)
        high_rows = jnp.where(at_high, high_value, 0.0).astype(BF16)
        low_rows = jnp.where(at_high, low_value, 0.0).astype(BF16)
        high_total += lax.dot_general(high_rows, at_low, NT_DIMS, preferred_element_type=F32)
        low_total += lax.dot_general(low_rows, at_low, NT_DIMS, preferred_element_type=F32)
    found = (high_total * 64.0 + low_total).astype(jnp.int32)
    inverse_ref[...] = jnp.clip(found, 0, perm_ref.shape[1] - 1)


def kernel(
    count,
    groups,
    q_hbm,
    k_hbm,
    v_hbm,
    g_hbm,
    perm,
    lists,
    pair_bias,
    inverse,
    hot,
    o_ref,
    dq_ref,
    dk_ref,
    dv_ref,
    bias_out_ref,
    q_in,
    k_in,
    v_in,
    g_in,
    send_whole,
    land_whole,
    send_half,
    land_half,
    wide,
    rows_0,
    rows_1,
    rows_2,
    rows_3,
    key_query,
    key_t,
    query_t,
    query_low,
    value,
    value_t,
    grad_t,
    grad_low,
    scores,
    grads,
    probs,
    run_tile,
    run_row,
    bias_pairs,
    bias_own,
    bias_groups,
    bias_sum,
    bias_heads,
    local_sem,
    send_sem,
    recv_sem,
):
    me = lax.axis_index("seq")
    group = lax.axis_index("dp")
    tiles = key_query.shape[0]
    pairs = scores.shape[0]
    low = lanes_low()
    low_half = low[:64]
    rows_of = (rows_0, rows_1, rows_2, rows_3)
    run_key = grads
    low_grads = probs

    def peer(step):
        return lax.rem(me + step, count)

    def group_peer(step):
        return lax.rem(group + step, groups)

    def stage(number, source, target):
        return pltpu.make_async_copy(source, target, local_sem.at[number])

    staged = [
        stage(number, source, target)
        for number, (source, target) in enumerate(
            (
                (k_hbm, k_in),
                (q_hbm, q_in),
                (v_hbm, v_in),
                (g_hbm, g_in),
            )
        )
    ]
    for copy in staged:
        copy.start()

    barrier = pltpu.get_barrier_semaphore()

    @pl.loop(1, count)
    def _(step):
        pl.semaphore_signal(barrier, inc=1, device_id=(group, peer(step)), device_id_type=MESH)

    @pl.loop(1, groups)
    def _(step):
        pl.semaphore_signal(barrier, inc=1, device_id=(group_peer(step), me), device_id_type=MESH)

    def remote(src, dst, which, other, other_group):
        return pltpu.make_async_remote_copy(
            src_ref=src,
            dst_ref=dst,
            send_sem=send_sem.at[which],
            recv_sem=recv_sem.at[which],
            device_id=(other_group, other),
            device_id_type=MESH,
        )

    KEY_QUERY, VALUE, GRAD, OUT, VALUE_GRAD, KEY_QUERY_GRAD = range(6)
    buffers = {
        KEY_QUERY: (send_whole.at[0], land_whole.at[0]),
        VALUE: (send_half.at[0], land_half.at[0]),
        GRAD: (send_half.at[1], land_half.at[1]),
        OUT: (send_half.at[2], land_half.at[2]),
        VALUE_GRAD: (send_half.at[3], land_half.at[3]),
        KEY_QUERY_GRAD: (send_whole.at[1], land_whole.at[1]),
    }

    def send_block(which, other):
        out, landing = buffers[which]
        remote(out.at[other], landing.at[me], which, other, group).start()

    def keep_own(which):
        out, landing = buffers[which]
        landing[me] = out[me]

    def all_blocks(which):
        out, landing = buffers[which]
        blocks = pl.ds(0, count - 1)
        return remote(out.at[blocks], landing.at[blocks], which, peer(1), group)

    def send_all(which):
        @pl.loop(1, count)
        def _(step):
            send_block(which, peer(step))

        keep_own(which)

    def columns_of(pair):
        return pl.ds(pl.multiple_of(pair * TILE, TILE), TILE)

    def rows_at(tile):
        return pl.ds(pl.multiple_of(tile * TILE, TILE), TILE)

    def pack(first_ref, second_ref, which):
        out, _ = buffers[which]

        def one(pair):
            columns = columns_of(pair)
            first, second = first_ref[0, :, columns], second_ref[0, :, columns]
            out[2 * pair] = jnp.where(low, first, rolled(second))
            out[2 * pair + 1] = jnp.where(low, rolled(first), second)

        unrolled(count // 2, ABREAST, one)

    def pack_half(source, which):
        out, _ = buffers[which]

        def one(pair):
            columns = columns_of(pair)
            top, bottom = source[0, pl.ds(0, 64), columns], source[0, pl.ds(64, 64), columns]
            out[2 * pair] = jnp.where(low_half, top, rolled(bottom))
            out[2 * pair + 1] = jnp.where(low_half, rolled(top), bottom)

        unrolled(count // 2, ABREAST, one)

    staged[0].wait()
    staged[1].wait()
    pack(k_in, q_in, KEY_QUERY)
    pl.semaphore_wait(barrier, count + groups - 2)
    send_all(KEY_QUERY)
    staged[2].wait()
    pack_half(v_in, VALUE)
    send_all(VALUE)
    staged[3].wait()
    pack_half(g_in, GRAD)
    send_all(GRAD)

    def cluster(use):
        @pl.loop(0, tiles // ABREAST)
        def _(step):
            for u in range(ABREAST):
                base = (step * ABREAST + u) * TILE
                gather_rows(wide, rows_of[u], lambda r, base=base: perm[0, base + r])
            for u in range(ABREAST):
                use(step * ABREAST + u, rows_of[u][...])

    def widen(which):
        landing = buffers[which][1]

        def one(block):
            wide[rows_at(block), :] = landing[block].astype(F32)

        unrolled(count, ABREAST, one)

    def widen_half(which):
        landing = buffers[which][1]

        def one(block):
            both = landing[block].astype(F32)
            wide[rows_at(block), :] = jnp.concatenate([both, pltpu.roll(both, 64, 1)], axis=0)

        unrolled(count, ABREAST, one)

    empty = jnp.zeros((64, TILE), F32)

    def use_key_query(tile, block):
        key_query[tile] = block.astype(BF16)
        turned = block.T
        key_t[tile] = turned[:64].astype(BF16)
        query_t[tile] = jnp.concatenate([turned[64:] * 0.125, empty], axis=0).astype(BF16)
        query_low[tile] = pltpu.roll(jnp.where(low, 0.0, block * 0.125), 64, 1).astype(BF16)

    all_blocks(KEY_QUERY).wait_recv()
    widen(KEY_QUERY)
    cluster(use_key_query)

    def first_of(row, p):
        return (p == 0) | (lists[row, p] != lists[row, jnp.maximum(p - 1, 0)])

    def over_pairs(start, body):
        def chunk(step, carry):
            for u in range(UNROLL):
                carry = body(step * UNROLL + u, carry)
            return carry

        lax.fori_loop(0, pairs // UNROLL, chunk, start)

    none = jnp.zeros((8, TILE), F32)

    def score_pair(p, peak):
        t, j = lists[T_OF, p], lists[J_OF, p]
        product = jnp.dot(key_query[j], query_t[t], preferred_element_type=F32)
        score = product * LOG2E + pair_bias[0, p]
        scores[p] = score
        before = jnp.where(first_of(T_OF, p), -jnp.inf, peak)
        peak = jnp.maximum(before, jnp.max(folded(score), axis=0))
        run_row[p] = peak
        return peak

    over_pairs(none, score_pair)
    run_row[...] = jnp.broadcast_to(jnp.max(run_row[...], axis=1, keepdims=True), run_row.shape)

    def power_pair(p, total):
        end = lists[T_LAST, lists[T_OF, p]]
        power = jnp.exp2(folded(scores[p]) - run_row[end][None])
        scores[p] = power.reshape(TILE, TILE)
        total = jnp.where(first_of(T_OF, p), 0.0, total) + jnp.sum(power, axis=0)
        bias_pairs[p] = total
        return total

    over_pairs(none, power_pair)
    bias_pairs[...] = jnp.broadcast_to(
        1.0 / jnp.sum(bias_pairs[...], axis=1, keepdims=True), bias_pairs.shape
    )

    def prob_pair(p, carry):
        end = lists[T_LAST, lists[T_OF, p]]
        prob = (folded(scores[p]) * bias_pairs[end][None]).reshape(TILE, TILE)
        scores[p] = prob
        probs[p] = prob.astype(BF16)
        return carry

    over_pairs(jnp.int32(0), prob_pair)

    def by_query_tile(left, right):
        def body(p, total):
            part = jnp.dot(left[lists[J_OF, p]], right[p], preferred_element_type=F32)
            total = jnp.where(first_of(T_OF, p), 0.0, total) + part
            run_tile[p] = total
            return total

        over_pairs(empty, body)

    def by_key_tile(left, right):
        def body(q, total):
            part = jnp.dot(
                left[lists[P_OF, q]], right[lists[TQ_OF, q]], preferred_element_type=F32
            )
            total = jnp.where(first_of(JQ_OF, q), 0.0, total) + part
            run_key[q] = total
            return total

        over_pairs(jnp.zeros((TILE, TILE), F32), body)

    def send_wide(which, half):
        out, _ = buffers[which]

        @pl.loop(0, count // ABREAST)
        def _(turn):
            for u in range(ABREAST):
                other = peer(turn * ABREAST + u + 1)
                gather_rows(
                    wide,
                    rows_of[u],
                    lambda r, other=other: inverse[2 * other + r // 64, r % 64],
                )
            for u in range(ABREAST):
                other = peer(turn * ABREAST + u + 1)
                block = rows_of[u][...]
                if half:
                    block = jnp.where(low_half, block[:64], pltpu.roll(block[64:], 64, 1))
                out[other] = block.astype(BF16)
            for u in range(ABREAST):
                step = turn * ABREAST + u + 1
                if u < ABREAST - 1:
                    send_block(which, peer(step))
                else:

                    @pl.when(step < count)
                    def _():
                        send_block(which, peer(step))

        keep_own(which)

    def use_value(tile, block):
        value[tile] = block.astype(BF16)
        value_t[tile] = block.T[:64].astype(BF16)

    all_blocks(VALUE).wait_recv()
    widen_half(VALUE)
    cluster(use_value)
    by_query_tile(value_t, probs)

    def turn_out(tile):
        of_query = run_tile[lists[T_LAST, tile]]
        wide[rows_at(tile), :] = jnp.concatenate([of_query, empty], axis=0).T

    unrolled(tiles, ABREAST, turn_out)
    send_wide(OUT, True)

    def use_grad(tile, block):
        grad_low[tile] = jnp.where(low, block, 0.0).astype(BF16)
        grad_t[tile] = jnp.concatenate([block.T[:64], empty], axis=0).astype(BF16)

    all_blocks(GRAD).wait_recv()
    widen_half(GRAD)
    cluster(use_grad)
    by_key_tile(probs, grad_low)

    def place_value_grad(tile):
        wide[rows_at(tile), :] = run_key[lists[J_LAST, tile]]

    unrolled(tiles, ABREAST, place_value_grad)
    send_wide(VALUE_GRAD, True)

    def prob_grad_pair(p, dots):
        t, j = lists[T_OF, p], lists[J_OF, p]
        product = jnp.dot(value[j], grad_t[t], preferred_element_type=F32)
        grads[p] = product
        dots = jnp.where(first_of(T_OF, p), 0.0, dots) + jnp.sum(
            folded(scores[p]) * folded(product), axis=0
        )
        run_row[p] = dots
        return dots

    over_pairs(none, prob_grad_pair)
    run_row[...] = jnp.broadcast_to(jnp.sum(run_row[...], axis=1, keepdims=True), run_row.shape)

    def score_grad_pair(p, carry):
        end = lists[T_LAST, lists[T_OF, p]]
        grad = folded(scores[p]) * (folded(grads[p]) - run_row[end][None])
        bias_pairs[p] = jnp.sum(grad, axis=0)
        low_grads[p] = grad.reshape(TILE, TILE).astype(BF16)
        return carry

    over_pairs(jnp.int32(0), score_grad_pair)
    by_query_tile(key_t, low_grads)
    by_key_tile(low_grads, query_low)

    def place_key_query_grad(tile):
        of_query = run_tile[lists[T_LAST, tile]] * 0.125
        of_key = run_key[lists[J_LAST, tile]]
        wide[rows_at(tile), :] = jnp.concatenate([empty, of_query], axis=0).T + of_key

    unrolled(tiles, ABREAST, place_key_query_grad)

    left = jnp.sum(bias_pairs[...], axis=1)
    class_sums = jnp.zeros((hot.shape[0], TILE), F32)
    hot_low = hot[...].astype(BF16)
    for _ in range(3):
        part = left.astype(BF16)
        class_sums += jnp.dot(hot_low, part, preferred_element_type=F32)
        left = left - part.astype(F32)
    own_column = iota(bias_own.shape, 1) == me
    bias_own[...] = jnp.where(own_column, jnp.sum(class_sums, axis=1, keepdims=True), 0.0)

    @pl.loop(1, groups)
    def _(step):
        remote(bias_own, bias_groups.at[group], 6, me, group_peer(step)).start()

    bias_groups[group] = bias_own[...]
    send_wide(KEY_QUERY_GRAD, False)

    own_groups = pl.ds(0, groups - 1)
    group_copies = remote(
        bias_groups.at[own_groups], bias_groups.at[own_groups], 6, me, group_peer(1)
    )
    group_copies.wait_recv()
    bias_sum[...] = jnp.sum(bias_groups[...], axis=0)

    @pl.loop(1, count)
    def _(step):
        remote(bias_sum, bias_heads.at[me], 7, peer(step), group).start()

    bias_heads[me] = bias_sum[...]

    def unpack_half(which, target):
        landing = buffers[which][1]

        def one(pair):
            even, odd = landing[2 * pair], landing[2 * pair + 1]
            target[pl.ds(0, 64), columns_of(pair)] = jnp.where(low_half, even, rolled(odd))
            target[pl.ds(64, 64), columns_of(pair)] = jnp.where(low_half, rolled(even), odd)

        unrolled(count // 2, ABREAST, one)

    def unpack(which, first_ref, second_ref):
        landing = buffers[which][1]

        def one(pair):
            even, odd = landing[2 * pair], landing[2 * pair + 1]
            first_ref[:, columns_of(pair)] = jnp.where(low, even, rolled(odd))
            second_ref[:, columns_of(pair)] = jnp.where(low, rolled(even), odd)

        unrolled(count // 2, ABREAST, one)

    all_blocks(OUT).wait_recv()
    unpack_half(OUT, o_ref)
    all_blocks(VALUE_GRAD).wait_recv()
    unpack_half(VALUE_GRAD, dv_ref)
    own_heads = pl.ds(0, count - 1)
    head_copies = remote(bias_heads.at[own_heads], bias_heads.at[own_heads], 7, peer(1), group)
    head_copies.wait_recv()
    bias_out_ref[...] = jnp.sum(bias_heads[...], axis=0)[:, : bias_out_ref.shape[1]]
    for which in (KEY_QUERY, VALUE, GRAD, OUT, VALUE_GRAD):
        all_blocks(which).wait_send()
    group_copies.wait_send()
    head_copies.wait_send()
    all_blocks(KEY_QUERY_GRAD).wait_recv()
    unpack(KEY_QUERY_GRAD, dk_ref, dq_ref)
    all_blocks(KEY_QUERY_GRAD).wait_send()


def plan(perm_ref, ids_ref, counts_ref, class_ref, bias_ref, list_ref, pair_bias_ref, inverse_ref, hot_ref):
    head = lax.axis_index("seq")
    write_lists(head, ids_ref, counts_ref, class_ref, bias_ref, list_ref, pair_bias_ref, hot_ref)
    write_inverse(perm_ref, inverse_ref)


def write_out(*refs):
    sources, targets, sems = refs[:5], refs[5:10], refs[10]
    copies = []
    for number, (source, target) in enumerate(zip(sources, targets)):
        place = target if number == 4 else target.at[0]
        copies.append(pltpu.make_async_copy(source, place, sems.at[number]))
    for copy in copies:
        copy.start()
    for copy in copies:
        copy.wait()


def local(
    queries, keys, values, out_grad, cluster_perm, tile_ids, tile_counts, hop_class, hop_bias
):
    count, groups = lax.axis_size("seq"), lax.axis_size("dp")
    nodes = cluster_perm.shape[1]
    tiles = nodes // TILE
    columns = queries.shape[2]
    classes, heads = hop_bias.shape
    pairs = TILE
    i32 = jnp.int32
    any_space = pl.BlockSpec(memory_space=pl.ANY)
    vmem = pl.BlockSpec(memory_space=pltpu.VMEM)
    smem = pl.BlockSpec(memory_space=pltpu.SMEM)
    one_output = jax.ShapeDtypeStruct((TILE, columns), BF16)
    bias_output = jax.ShapeDtypeStruct((classes, heads), F32)
    tile_blocks = pltpu.VMEM((tiles, TILE, TILE), BF16)
    half_blocks = pltpu.VMEM((tiles, 64, TILE), BF16)

    lists, pair_bias, inverse, hot = pl.pallas_call(
        plan,
        out_shape=(
            jax.ShapeDtypeStruct((8, TILE), i32),
            jax.ShapeDtypeStruct((8, TILE), F32),
            jax.ShapeDtypeStruct((64, 64), i32),
            jax.ShapeDtypeStruct((classes, TILE), F32),
        ),
        in_specs=[vmem] * 5,
        out_specs=(vmem,) * 4,
        compiler_params=pltpu.CompilerParams(vmem_limit_bytes=4 << 20),
        name="plan",
    )(
        cluster_perm,
        jnp.swapaxes(tile_ids, 1, 2),
        tile_counts,
        jnp.swapaxes(hop_class, 1, 2),
        hop_bias,
    )

    results = pl.pallas_call(
        functools.partial(kernel, count, groups),
        out_shape=(one_output,) * 4 + (bias_output,),
        in_specs=[any_space] * 4 + [smem] * 4 + [vmem],
        out_specs=(vmem,) * 5,
        scratch_shapes=[pltpu.VMEM((1, TILE, columns), BF16)] * 4
        + [
            pltpu.VMEM((2, count, TILE, TILE), BF16),
            pltpu.VMEM((2, count, TILE, TILE), BF16),
            pltpu.VMEM((4, count, 64, TILE), BF16),
            pltpu.VMEM((4, count, 64, TILE), BF16),
            pltpu.VMEM((nodes, TILE), F32),
        ]
        + [pltpu.VMEM((TILE, TILE), F32)] * 4
        + [
            tile_blocks,
            half_blocks,
            tile_blocks,
            tile_blocks,
            tile_blocks,
            half_blocks,
            tile_blocks,
            tile_blocks,
            pltpu.VMEM((pairs, TILE, TILE), F32),
            pltpu.VMEM((pairs, TILE, TILE), F32),
            pltpu.VMEM((pairs, TILE, TILE), BF16),
            pltpu.VMEM((pairs, 64, TILE), F32),
            pltpu.VMEM((pairs, 8, TILE), F32),
            pltpu.VMEM((pairs, 8, TILE), F32),
            pltpu.VMEM((classes, TILE), F32),
            pltpu.VMEM((groups, classes, TILE), F32),
            pltpu.VMEM((classes, TILE), F32),
            pltpu.VMEM((count, classes, TILE), F32),
            pltpu.SemaphoreType.DMA((4,)),
            pltpu.SemaphoreType.DMA((8,)),
            pltpu.SemaphoreType.DMA((8,)),
        ],
        compiler_params=pltpu.CompilerParams(
            collective_id=0, has_side_effects=True, vmem_limit_bytes=51 << 20
        ),
        name="graph_attention",
    )(
        queries,
        keys,
        values,
        out_grad,
        cluster_perm,
        lists,
        pair_bias,
        inverse,
        hot,
    )

    whole_output = jax.ShapeDtypeStruct((1, TILE, columns), BF16)
    return pl.pallas_call(
        write_out,
        out_shape=(whole_output,) * 4 + (bias_output,),
        in_specs=[vmem] * 5,
        out_specs=(any_space,) * 5,
        scratch_shapes=[pltpu.SemaphoreType.DMA((5,))],
        compiler_params=pltpu.CompilerParams(vmem_limit_bytes=1 << 20),
        name="write_out",
    )(*results)


def solution(mesh):
    wide = P("dp", "seq", None)
    return jax.shard_map(
        local,
        mesh=mesh,
        in_specs=(
            wide,
            wide,
            wide,
            wide,
            P("dp", None),
            P("dp", None, None),
            P("dp", None),
            P("dp", None, None),
            P(),
        ),
        out_specs=(wide, wide, wide, wide, P()),
        check_vma=False,
    )
```

```python
import functools
import math

import jax
import jax.numpy as jnp
from jax import lax
from jax.experimental import pallas as pl
from jax.experimental.pallas import tpu as pltpu
from jax.sharding import PartitionSpec as P

MESH = pl.DeviceIdType.MESH
TILE = 128
LOG2E = math.log2(math.e)
NT_DIMS = (((1,), (1,)), ((), ()))
BF16, F32 = jnp.bfloat16, jnp.float32
UNROLL = 32
ABREAST = 4

T_OF, J_OF, P_OF, TQ_OF, JQ_OF, T_LAST, J_LAST = range(7)


def iota(shape, axis):
    return lax.broadcasted_iota(jnp.int32, shape, axis)


def lanes_low():
    return iota((TILE, TILE), 1) < 64


def rolled(block):
    return pltpu.roll(block.astype(F32), 64, 1).astype(BF16)


def folded(block):
    return block.reshape(TILE // 8, 8, TILE)


def gather_rows(source, rows_out, index_of):
    for r in range(TILE):
        rows_out[pl.ds(r, 1), :] = source[pl.ds(index_of(r), 1), :]


def unrolled(count, factor, body):
    def turn(step, carry):
        for u in range(factor):
            body(step * factor + u)
        return carry

    lax.fori_loop(0, count // factor, turn, jnp.int32(0))


def write_lists(head, ids_ref, counts_ref, class_ref, bias_ref, list_ref, pair_bias_ref, hot_ref):
    slots, tiles = ids_ref.shape[1], ids_ref.shape[2]
    flat = tiles * slots
    lane_slot = iota((tiles, flat), 1) % slots
    own = iota((tiles, flat), 1) // slots == iota((tiles, flat), 0)

    diagonal = iota((tiles, tiles), 0) == iota((tiles, tiles), 1)

    def upright(row):
        return jnp.sum(jnp.where(diagonal, row, 0.0), axis=1, keepdims=True)

    def flat_row(table):
        spread = jnp.zeros((tiles, flat), F32)
        for s in range(slots):
            spread = jnp.where(lane_slot == s, upright(table[s : s + 1, :]), spread)
        return jnp.sum(jnp.where(own, spread, 0.0), axis=0, keepdims=True)

    def column(row):
        return jnp.broadcast_to(row, (TILE, flat)).T

    counts = upright(counts_ref[...].astype(F32))
    used = jnp.sum(
        jnp.where(own & (lane_slot.astype(F32) < counts), 1.0, 0.0), axis=0, keepdims=True
    )
    tile_row = flat_row(ids_ref[0].astype(F32))
    class_row = flat_row(class_ref[0].astype(F32))
    used_col, tile_col, class_col = column(used), column(tile_row), column(class_row)
    place = iota((flat, TILE), 0)
    place_wide = place.astype(F32)
    query_col = (place // slots).astype(F32)
    lane = iota((flat, TILE), 1).astype(F32)

    def ranks(key_col, key_row):
        parts = []
        for start in range(0, flat, TILE):
            before = (used_col > 0.5) & (key_col < key_row[:, start : start + TILE])
            parts.append(jnp.sum(jnp.where(before, 1.0, 0.0), axis=0, keepdims=True))
        return column(jnp.concatenate(parts, axis=1))

    place_row = iota((1, flat), 1).astype(F32)
    by_query = ranks(place_wide, place_row)
    by_key = ranks(tile_col * flat + place_wide, tile_row * flat + place_row)

    def pick(rank, values):
        return jnp.sum(
            jnp.where((rank == lane) & (used_col > 0.5), values, 0.0), axis=0, keepdims=True
        )

    def last(values):
        reached = (used_col > 0.5) & (values <= lane)
        return jnp.sum(jnp.where(reached, 1.0, 0.0), axis=0, keepdims=True) - 1.0

    class_of = pick(by_query, class_col)
    rows = (
        pick(by_query, query_col),
        pick(by_query, tile_col),
        pick(by_key, by_query),
        pick(by_key, query_col),
        pick(by_key, tile_col),
        last(query_col),
        last(tile_col),
    )
    table = jnp.concatenate(rows + (jnp.zeros((8 - len(rows), TILE), F32),), axis=0)
    list_ref[...] = jnp.clip(table.astype(jnp.int32), 0, TILE - 1)

    classes, heads = bias_ref.shape
    hot = jnp.where(iota((classes, TILE), 0).astype(F32) == class_of, 1.0, 0.0)
    hot_ref[...] = hot
    own_bias = jnp.sum(
        jnp.where(iota((classes, heads), 1) == head, bias_ref[...], 0.0), axis=1, keepdims=True
    )
    pair_bias = jnp.sum(hot * own_bias, axis=0, keepdims=True) * LOG2E
    pair_bias_ref[...] = jnp.broadcast_to(pair_bias, pair_bias_ref.shape)


def write_inverse(perm_ref, inverse_ref):
    high_total = jnp.zeros((64, 64), F32)
    low_total = jnp.zeros((64, 64), F32)
    width = 1024
    for start in range(0, perm_ref.shape[1], width):
        node = perm_ref[:, pl.ds(start, width)]
        digit = iota((64, width), 0)
        position = iota((64, width), 1) + start
        at_high = lax.shift_right_logical(node, 6) == digit
        at_low = jnp.where((node & 63) == digit, 1.0, 0.0).astype(BF16)
        high_value = lax.shift_right_logical(position, 6).astype(F32)
        low_value = (position & 63).astype(F32)
        high_rows = jnp.where(at_high, high_value, 0.0).astype(BF16)
        low_rows = jnp.where(at_high, low_value, 0.0).astype(BF16)
        high_total += lax.dot_general(high_rows, at_low, NT_DIMS, preferred_element_type=F32)
        low_total += lax.dot_general(low_rows, at_low, NT_DIMS, preferred_element_type=F32)
    found = (high_total * 64.0 + low_total).astype(jnp.int32)
    inverse_ref[...] = jnp.clip(found, 0, perm_ref.shape[1] - 1)


def kernel(
    count,
    groups,
    q_hbm,
    k_hbm,
    v_hbm,
    g_hbm,
    perm_hbm,
    lists_hbm,
    pair_bias_hbm,
    inverse_hbm,
    hot_hbm,
    o_ref,
    dq_ref,
    dk_ref,
    dv_ref,
    bias_out_ref,
    q_in,
    k_in,
    v_in,
    g_in,
    perm,
    lists,
    pair_bias,
    inverse,
    hot,
    send_whole,
    land_whole,
    send_half,
    land_half,
    wide,
    rows_0,
    rows_1,
    rows_2,
    rows_3,
    key_query,
    key_t,
    query_t,
    query_low,
    value,
    value_t,
    grad_t,
    grad_low,
    scores,
    grads,
    probs,
    run_tile,
    run_row,
    bias_pairs,
    bias_own,
    bias_groups,
    bias_sum,
    bias_heads,
    local_sem,
    send_sem,
    recv_sem,
):
    me = lax.axis_index("seq")
    group = lax.axis_index("dp")
    tiles = key_query.shape[0]
    pairs = scores.shape[0]
    low = lanes_low()
    low_half = low[:64]
    rows_of = (rows_0, rows_1, rows_2, rows_3)
    run_key = grads
    low_grads = probs

    def peer(step):
        return lax.rem(me + step, count)

    def group_peer(step):
        return lax.rem(group + step, groups)

    def stage(number, source, target):
        return pltpu.make_async_copy(source, target, local_sem.at[number])

    staged = [
        stage(number, source, target)
        for number, (source, target) in enumerate(
            (
                (k_hbm, k_in),
                (q_hbm, q_in),
                (v_hbm, v_in),
                (g_hbm, g_in),
                (perm_hbm, perm),
                (lists_hbm, lists),
                (pair_bias_hbm, pair_bias),
                (inverse_hbm, inverse),
                (hot_hbm, hot),
            )
        )
    ]
    for copy in staged:
        copy.start()

    barrier = pltpu.get_barrier_semaphore()

    @pl.loop(1, count)
    def _(step):
        pl.semaphore_signal(barrier, inc=1, device_id=(group, peer(step)), device_id_type=MESH)

    @pl.loop(1, groups)
    def _(step):
        pl.semaphore_signal(barrier, inc=1, device_id=(group_peer(step), me), device_id_type=MESH)

    def remote(src, dst, which, other, other_group):
        return pltpu.make_async_remote_copy(
            src_ref=src,
            dst_ref=dst,
            send_sem=send_sem.at[which],
            recv_sem=recv_sem.at[which],
            device_id=(other_group, other),
            device_id_type=MESH,
        )

    KEY_QUERY, VALUE, GRAD, OUT, VALUE_GRAD, KEY_QUERY_GRAD = range(6)
    buffers = {
        KEY_QUERY: (send_whole.at[0], land_whole.at[0]),
        VALUE: (send_half.at[0], land_half.at[0]),
        GRAD: (send_half.at[1], land_half.at[1]),
        OUT: (send_half.at[2], land_half.at[2]),
        VALUE_GRAD: (send_half.at[3], land_half.at[3]),
        KEY_QUERY_GRAD: (send_whole.at[1], land_whole.at[1]),
    }

    def send_block(which, other):
        out, landing = buffers[which]
        remote(out.at[other], landing.at[me], which, other, group).start()

    def keep_own(which):
        out, landing = buffers[which]
        landing[me] = out[me]

    def all_blocks(which):
        out, landing = buffers[which]
        blocks = pl.ds(0, count - 1)
        return remote(out.at[blocks], landing.at[blocks], which, peer(1), group)

    def send_all(which):
        @pl.loop(1, count)
        def _(step):
            send_block(which, peer(step))

        keep_own(which)

    def columns_of(pair):
        return pl.ds(pl.multiple_of(pair * TILE, TILE), TILE)

    def rows_at(tile):
        return pl.ds(pl.multiple_of(tile * TILE, TILE), TILE)

    def pack(first_ref, second_ref, which):
        out, _ = buffers[which]

        def one(pair):
            columns = columns_of(pair)
            first, second = first_ref[0, :, columns], second_ref[0, :, columns]
            out[2 * pair] = jnp.where(low, first, rolled(second))
            out[2 * pair + 1] = jnp.where(low, rolled(first), second)

        unrolled(count // 2, ABREAST, one)

    def pack_half(source, which):
        out, _ = buffers[which]

        def one(pair):
            columns = columns_of(pair)
            top, bottom = source[0, pl.ds(0, 64), columns], source[0, pl.ds(64, 64), columns]
            out[2 * pair] = jnp.where(low_half, top, rolled(bottom))
            out[2 * pair + 1] = jnp.where(low_half, rolled(top), bottom)

        unrolled(count // 2, ABREAST, one)

    staged[0].wait()
    staged[1].wait()
    pack(k_in, q_in, KEY_QUERY)
    pl.semaphore_wait(barrier, count + groups - 2)
    send_all(KEY_QUERY)
    staged[2].wait()
    pack_half(v_in, VALUE)
    send_all(VALUE)
    staged[3].wait()
    pack_half(g_in, GRAD)
    send_all(GRAD)
    for copy in staged[4:]:
        copy.wait()

    def cluster(use):
        @pl.loop(0, tiles // ABREAST)
        def _(step):
            for u in range(ABREAST):
                base = (step * ABREAST + u) * TILE
                gather_rows(wide, rows_of[u], lambda r, base=base: perm[0, base + r])
            for u in range(ABREAST):
                use(step * ABREAST + u, rows_of[u][...])

    def widen(which):
        landing = buffers[which][1]

        def one(block):
            wide[rows_at(block), :] = landing[block].astype(F32)

        unrolled(count, ABREAST, one)

    def widen_half(which):
        landing = buffers[which][1]

        def one(block):
            both = landing[block].astype(F32)
            wide[rows_at(block), :] = jnp.concatenate([both, pltpu.roll(both, 64, 1)], axis=0)

        unrolled(count, ABREAST, one)

    empty = jnp.zeros((64, TILE), F32)

    def use_key_query(tile, block):
        key_query[tile] = block.astype(BF16)
        turned = block.T
        key_t[tile] = turned[:64].astype(BF16)
        query_t[tile] = jnp.concatenate([turned[64:] * 0.125, empty], axis=0).astype(BF16)
        query_low[tile] = pltpu.roll(jnp.where(low, 0.0, block * 0.125), 64, 1).astype(BF16)

    all_blocks(KEY_QUERY).wait_recv()
    widen(KEY_QUERY)
    cluster(use_key_query)

    def first_of(row, p):
        return (p == 0) | (lists[row, p] != lists[row, jnp.maximum(p - 1, 0)])

    def over_pairs(start, body):
        def chunk(step, carry):
            for u in range(UNROLL):
                carry = body(step * UNROLL + u, carry)
            return carry

        lax.fori_loop(0, pairs // UNROLL, chunk, start)

    none = jnp.zeros((8, TILE), F32)

    def score_pair(p, peak):
        t, j = lists[T_OF, p], lists[J_OF, p]
        product = jnp.dot(key_query[j], query_t[t], preferred_element_type=F32)
        score = product * LOG2E + pair_bias[0, p]
        scores[p] = score
        before = jnp.where(first_of(T_OF, p), -jnp.inf, peak)
        peak = jnp.maximum(before, jnp.max(folded(score), axis=0))
        run_row[p] = peak
        return peak

    over_pairs(none, score_pair)
    run_row[...] = jnp.broadcast_to(jnp.max(run_row[...], axis=1, keepdims=True), run_row.shape)

    def power_pair(p, total):
        end = lists[T_LAST, lists[T_OF, p]]
        power = jnp.exp2(folded(scores[p]) - run_row[end][None])
        scores[p] = power.reshape(TILE, TILE)
        total = jnp.where(first_of(T_OF, p), 0.0, total) + jnp.sum(power, axis=0)
        bias_pairs[p] = total
        return total

    over_pairs(none, power_pair)
    bias_pairs[...] = jnp.broadcast_to(
        1.0 / jnp.sum(bias_pairs[...], axis=1, keepdims=True), bias_pairs.shape
    )

    def prob_pair(p, carry):
        end = lists[T_LAST, lists[T_OF, p]]
        prob = (folded(scores[p]) * bias_pairs[end][None]).reshape(TILE, TILE)
        scores[p] = prob
        probs[p] = prob.astype(BF16)
        return carry

    over_pairs(jnp.int32(0), prob_pair)

    def by_query_tile(left, right):
        def body(p, total):
            part = jnp.dot(left[lists[J_OF, p]], right[p], preferred_element_type=F32)
            total = jnp.where(first_of(T_OF, p), 0.0, total) + part
            run_tile[p] = total
            return total

        over_pairs(empty, body)

    def by_key_tile(left, right):
        def body(q, total):
            part = jnp.dot(
                left[lists[P_OF, q]], right[lists[TQ_OF, q]], preferred_element_type=F32
            )
            total = jnp.where(first_of(JQ_OF, q), 0.0, total) + part
            run_key[q] = total
            return total

        over_pairs(jnp.zeros((TILE, TILE), F32), body)

    def send_wide(which, half):
        out, _ = buffers[which]

        @pl.loop(0, count // ABREAST)
        def _(turn):
            for u in range(ABREAST):
                other = peer(turn * ABREAST + u + 1)
                gather_rows(
                    wide,
                    rows_of[u],
                    lambda r, other=other: inverse[2 * other + r // 64, r % 64],
                )
            for u in range(ABREAST):
                other = peer(turn * ABREAST + u + 1)
                block = rows_of[u][...]
                if half:
                    block = jnp.where(low_half, block[:64], pltpu.roll(block[64:], 64, 1))
                out[other] = block.astype(BF16)
            for u in range(ABREAST):
                step = turn * ABREAST + u + 1
                if u < ABREAST - 1:
                    send_block(which, peer(step))
                else:

                    @pl.when(step < count)
                    def _():
                        send_block(which, peer(step))

        keep_own(which)

    def use_value(tile, block):
        value[tile] = block.astype(BF16)
        value_t[tile] = block.T[:64].astype(BF16)

    all_blocks(VALUE).wait_recv()
    widen_half(VALUE)
    cluster(use_value)
    by_query_tile(value_t, probs)

    def turn_out(tile):
        of_query = run_tile[lists[T_LAST, tile]]
        wide[rows_at(tile), :] = jnp.concatenate([of_query, empty], axis=0).T

    unrolled(tiles, ABREAST, turn_out)
    send_wide(OUT, True)

    def use_grad(tile, block):
        grad_low[tile] = jnp.where(low, block, 0.0).astype(BF16)
        grad_t[tile] = jnp.concatenate([block.T[:64], empty], axis=0).astype(BF16)

    all_blocks(GRAD).wait_recv()
    widen_half(GRAD)
    cluster(use_grad)
    by_key_tile(probs, grad_low)

    def place_value_grad(tile):
        wide[rows_at(tile), :] = run_key[lists[J_LAST, tile]]

    unrolled(tiles, ABREAST, place_value_grad)
    send_wide(VALUE_GRAD, True)

    def prob_grad_pair(p, dots):
        t, j = lists[T_OF, p], lists[J_OF, p]
        product = jnp.dot(value[j], grad_t[t], preferred_element_type=F32)
        grads[p] = product
        dots = jnp.where(first_of(T_OF, p), 0.0, dots) + jnp.sum(
            folded(scores[p]) * folded(product), axis=0
        )
        run_row[p] = dots
        return dots

    over_pairs(none, prob_grad_pair)
    run_row[...] = jnp.broadcast_to(jnp.sum(run_row[...], axis=1, keepdims=True), run_row.shape)

    def score_grad_pair(p, carry):
        end = lists[T_LAST, lists[T_OF, p]]
        grad = folded(scores[p]) * (folded(grads[p]) - run_row[end][None])
        bias_pairs[p] = jnp.sum(grad, axis=0)
        low_grads[p] = grad.reshape(TILE, TILE).astype(BF16)
        return carry

    over_pairs(jnp.int32(0), score_grad_pair)
    by_query_tile(key_t, low_grads)
    by_key_tile(low_grads, query_low)

    def place_key_query_grad(tile):
        of_query = run_tile[lists[T_LAST, tile]] * 0.125
        of_key = run_key[lists[J_LAST, tile]]
        wide[rows_at(tile), :] = jnp.concatenate([empty, of_query], axis=0).T + of_key

    unrolled(tiles, ABREAST, place_key_query_grad)

    left = jnp.sum(bias_pairs[...], axis=1)
    class_sums = jnp.zeros((hot.shape[0], TILE), F32)
    hot_low = hot[...].astype(BF16)
    for _ in range(3):
        part = left.astype(BF16)
        class_sums += jnp.dot(hot_low, part, preferred_element_type=F32)
        left = left - part.astype(F32)
    own_column = iota(bias_own.shape, 1) == me
    bias_own[...] = jnp.where(own_column, jnp.sum(class_sums, axis=1, keepdims=True), 0.0)

    @pl.loop(1, groups)
    def _(step):
        remote(bias_own, bias_groups.at[group], 6, me, group_peer(step)).start()

    bias_groups[group] = bias_own[...]
    send_wide(KEY_QUERY_GRAD, False)

    own_groups = pl.ds(0, groups - 1)
    group_copies = remote(
        bias_groups.at[own_groups], bias_groups.at[own_groups], 6, me, group_peer(1)
    )
    group_copies.wait_recv()
    bias_sum[...] = jnp.sum(bias_groups[...], axis=0)

    @pl.loop(1, count)
    def _(step):
        remote(bias_sum, bias_heads.at[me], 7, peer(step), group).start()

    bias_heads[me] = bias_sum[...]

    def unpack_half(which, target):
        landing = buffers[which][1]

        def one(pair):
            even, odd = landing[2 * pair], landing[2 * pair + 1]
            target[pl.ds(0, 64), columns_of(pair)] = jnp.where(low_half, even, rolled(odd))
            target[pl.ds(64, 64), columns_of(pair)] = jnp.where(low_half, rolled(even), odd)

        unrolled(count // 2, ABREAST, one)

    def unpack(which, first_ref, second_ref):
        landing = buffers[which][1]

        def one(pair):
            even, odd = landing[2 * pair], landing[2 * pair + 1]
            first_ref[:, columns_of(pair)] = jnp.where(low, even, rolled(odd))
            second_ref[:, columns_of(pair)] = jnp.where(low, rolled(even), odd)

        unrolled(count // 2, ABREAST, one)

    all_blocks(OUT).wait_recv()
    unpack_half(OUT, o_ref)
    all_blocks(VALUE_GRAD).wait_recv()
    unpack_half(VALUE_GRAD, dv_ref)
    own_heads = pl.ds(0, count - 1)
    head_copies = remote(bias_heads.at[own_heads], bias_heads.at[own_heads], 7, peer(1), group)
    head_copies.wait_recv()
    bias_out_ref[...] = jnp.sum(bias_heads[...], axis=0)[:, : bias_out_ref.shape[1]]
    for which in (KEY_QUERY, VALUE, GRAD, OUT, VALUE_GRAD):
        all_blocks(which).wait_send()
    group_copies.wait_send()
    head_copies.wait_send()
    all_blocks(KEY_QUERY_GRAD).wait_recv()
    unpack(KEY_QUERY_GRAD, dk_ref, dq_ref)
    all_blocks(KEY_QUERY_GRAD).wait_send()


def plan(perm_ref, ids_ref, counts_ref, class_ref, bias_ref, list_ref, pair_bias_ref, inverse_ref, hot_ref):
    head = lax.axis_index("seq")
    write_lists(head, ids_ref, counts_ref, class_ref, bias_ref, list_ref, pair_bias_ref, hot_ref)
    write_inverse(perm_ref, inverse_ref)


def write_out(*refs):
    sources, targets, sems = refs[:5], refs[5:10], refs[10]
    copies = []
    for number, (source, target) in enumerate(zip(sources, targets)):
        place = target if number == 4 else target.at[0]
        copies.append(pltpu.make_async_copy(source, place, sems.at[number]))
    for copy in copies:
        copy.start()
    for copy in copies:
        copy.wait()


def local(
    queries, keys, values, out_grad, cluster_perm, tile_ids, tile_counts, hop_class, hop_bias
):
    count, groups = lax.axis_size("seq"), lax.axis_size("dp")
    nodes = cluster_perm.shape[1]
    tiles = nodes // TILE
    columns = queries.shape[2]
    classes, heads = hop_bias.shape
    pairs = TILE
    i32 = jnp.int32
    any_space = pl.BlockSpec(memory_space=pl.ANY)
    vmem = pl.BlockSpec(memory_space=pltpu.VMEM)
    one_output = jax.ShapeDtypeStruct((TILE, columns), BF16)
    bias_output = jax.ShapeDtypeStruct((classes, heads), F32)
    tile_blocks = pltpu.VMEM((tiles, TILE, TILE), BF16)
    half_blocks = pltpu.VMEM((tiles, 64, TILE), BF16)

    lists, pair_bias, inverse, hot = pl.pallas_call(
        plan,
        out_shape=(
            jax.ShapeDtypeStruct((8, TILE), i32),
            jax.ShapeDtypeStruct((8, TILE), F32),
            jax.ShapeDtypeStruct((64, 64), i32),
            jax.ShapeDtypeStruct((classes, TILE), F32),
        ),
        in_specs=[vmem] * 5,
        out_specs=(vmem,) * 4,
        compiler_params=pltpu.CompilerParams(vmem_limit_bytes=4 << 20),
        name="plan",
    )(
        cluster_perm,
        jnp.swapaxes(tile_ids, 1, 2),
        tile_counts,
        jnp.swapaxes(hop_class, 1, 2),
        hop_bias,
    )

    results = pl.pallas_call(
        functools.partial(kernel, count, groups),
        out_shape=(one_output,) * 4 + (bias_output,),
        in_specs=[any_space] * 9,
        out_specs=(vmem,) * 5,
        scratch_shapes=[pltpu.VMEM((1, TILE, columns), BF16)] * 4
        + [
            pltpu.SMEM((1, nodes), i32),
            pltpu.SMEM((8, TILE), i32),
            pltpu.SMEM((8, TILE), F32),
            pltpu.SMEM((64, 64), i32),
            pltpu.VMEM((classes, TILE), F32),
            pltpu.VMEM((2, count, TILE, TILE), BF16),
            pltpu.VMEM((2, count, TILE, TILE), BF16),
            pltpu.VMEM((4, count, 64, TILE), BF16),
            pltpu.VMEM((4, count, 64, TILE), BF16),
            pltpu.VMEM((nodes, TILE), F32),
        ]
        + [pltpu.VMEM((TILE, TILE), F32)] * 4
        + [
            tile_blocks,
            half_blocks,
            tile_blocks,
            tile_blocks,
            tile_blocks,
            half_blocks,
            tile_blocks,
            tile_blocks,
            pltpu.VMEM((pairs, TILE, TILE), F32),
            pltpu.VMEM((pairs, TILE, TILE), F32),
            pltpu.VMEM((pairs, TILE, TILE), BF16),
            pltpu.VMEM((pairs, 64, TILE), F32),
            pltpu.VMEM((pairs, 8, TILE), F32),
            pltpu.VMEM((pairs, 8, TILE), F32),
            pltpu.VMEM((classes, TILE), F32),
            pltpu.VMEM((groups, classes, TILE), F32),
            pltpu.VMEM((classes, TILE), F32),
            pltpu.VMEM((count, classes, TILE), F32),
            pltpu.SemaphoreType.DMA((9,)),
            pltpu.SemaphoreType.DMA((8,)),
            pltpu.SemaphoreType.DMA((8,)),
        ],
        compiler_params=pltpu.CompilerParams(
            collective_id=0, has_side_effects=True, vmem_limit_bytes=103 << 19
        ),
        name="graph_attention",
    )(
        queries,
        keys,
        values,
        out_grad,
        cluster_perm,
        lists,
        pair_bias,
        inverse,
        hot,
    )

    whole_output = jax.ShapeDtypeStruct((1, TILE, columns), BF16)
    return pl.pallas_call(
        write_out,
        out_shape=(whole_output,) * 4 + (bias_output,),
        in_specs=[vmem] * 5,
        out_specs=(any_space,) * 5,
        scratch_shapes=[pltpu.SemaphoreType.DMA((5,))],
        compiler_params=pltpu.CompilerParams(vmem_limit_bytes=1 << 20),
        name="write_out",
    )(*results)


def solution(mesh):
    wide = P("dp", "seq", None)
    return jax.shard_map(
        local,
        mesh=mesh,
        in_specs=(
            wide,
            wide,
            wide,
            wide,
            P("dp", None),
            P("dp", None, None),
            P("dp", None),
            P("dp", None, None),
            P(),
        ),
        out_specs=(wide, wide, wide, wide, P()),
        check_vma=False,
    )
```

```python
import functools
import math

import jax
import jax.numpy as jnp
from jax import lax
from jax.experimental import pallas as pl
from jax.experimental.pallas import tpu as pltpu
from jax.sharding import PartitionSpec as P

MESH = pl.DeviceIdType.MESH
TILE = 128
LOG2E = math.log2(math.e)
NT_DIMS = (((1,), (1,)), ((), ()))
BF16, F32 = jnp.bfloat16, jnp.float32
UNROLL = 32
ABREAST = 4

T_OF, J_OF, P_OF, TQ_OF, JQ_OF, T_LAST, J_LAST, C_OF = range(8)


def iota(shape, axis):
    return lax.broadcasted_iota(jnp.int32, shape, axis)


def lanes_low():
    return iota((TILE, TILE), 1) < 64


def rolled(block):
    return pltpu.roll(block.astype(F32), 64, 1).astype(BF16)


def folded(block):
    return block.reshape(TILE // 8, 8, TILE)


def gather_rows(source, rows_out, index_of):
    for r in range(TILE):
        rows_out[pl.ds(r, 1), :] = source[pl.ds(index_of(r), 1), :]


def unrolled(count, factor, body):
    def turn(step, carry):
        for u in range(factor):
            body(step * factor + u)
        return carry

    lax.fori_loop(0, count // factor, turn, jnp.int32(0))


def write_lists(ids_ref, counts_ref, class_ref, list_ref, hot_ref):
    slots, tiles = ids_ref.shape[1], ids_ref.shape[2]
    flat = tiles * slots
    lane_slot = iota((tiles, flat), 1) % slots
    own = iota((tiles, flat), 1) // slots == iota((tiles, flat), 0)

    diagonal = iota((tiles, tiles), 0) == iota((tiles, tiles), 1)

    def upright(row):
        return jnp.sum(jnp.where(diagonal, row, 0.0), axis=1, keepdims=True)

    def flat_row(table):
        spread = jnp.zeros((tiles, flat), F32)
        for s in range(slots):
            spread = jnp.where(lane_slot == s, upright(table[s : s + 1, :]), spread)
        return jnp.sum(jnp.where(own, spread, 0.0), axis=0, keepdims=True)

    def column(row):
        return jnp.broadcast_to(row, (TILE, flat)).T

    counts = upright(counts_ref[...].astype(F32))
    used = jnp.sum(
        jnp.where(own & (lane_slot.astype(F32) < counts), 1.0, 0.0), axis=0, keepdims=True
    )
    tile_row = flat_row(ids_ref[0].astype(F32))
    class_row = flat_row(class_ref[0].astype(F32))
    used_col, tile_col, class_col = column(used), column(tile_row), column(class_row)
    place = iota((flat, TILE), 0)
    place_wide = place.astype(F32)
    query_col = (place // slots).astype(F32)
    lane = iota((flat, TILE), 1).astype(F32)

    def ranks(key_col, key_row):
        parts = []
        for start in range(0, flat, TILE):
            before = (used_col > 0.5) & (key_col < key_row[:, start : start + TILE])
            parts.append(jnp.sum(jnp.where(before, 1.0, 0.0), axis=0, keepdims=True))
        return column(jnp.concatenate(parts, axis=1))

    place_row = iota((1, flat), 1).astype(F32)
    by_query = ranks(place_wide, place_row)
    by_key = ranks(tile_col * flat + place_wide, tile_row * flat + place_row)

    def pick(rank, values):
        return jnp.sum(
            jnp.where((rank == lane) & (used_col > 0.5), values, 0.0), axis=0, keepdims=True
        )

    def last(values):
        reached = (used_col > 0.5) & (values <= lane)
        return jnp.sum(jnp.where(reached, 1.0, 0.0), axis=0, keepdims=True) - 1.0

    class_of = pick(by_query, class_col)
    rows = (
        pick(by_query, query_col),
        pick(by_query, tile_col),
        pick(by_key, by_query),
        pick(by_key, query_col),
        pick(by_key, tile_col),
        last(query_col),
        last(tile_col),
        class_of,
    )
    table = jnp.concatenate(rows, axis=0)
    list_ref[...] = jnp.clip(table.astype(jnp.int32), 0, TILE - 1)

    hot_ref[...] = jnp.where(iota(hot_ref.shape, 0).astype(F32) == class_of, 1.0, 0.0)


def write_inverse(perm_ref, inverse_ref):
    high_total = jnp.zeros((64, 64), F32)
    low_total = jnp.zeros((64, 64), F32)
    width = 1024
    for start in range(0, perm_ref.shape[1], width):
        node = perm_ref[:, pl.ds(start, width)]
        digit = iota((64, width), 0)
        position = iota((64, width), 1) + start
        at_high = lax.shift_right_logical(node, 6) == digit
        at_low = jnp.where((node & 63) == digit, 1.0, 0.0).astype(BF16)
        high_value = lax.shift_right_logical(position, 6).astype(F32)
        low_value = (position & 63).astype(F32)
        high_rows = jnp.where(at_high, high_value, 0.0).astype(BF16)
        low_rows = jnp.where(at_high, low_value, 0.0).astype(BF16)
        high_total += lax.dot_general(high_rows, at_low, NT_DIMS, preferred_element_type=F32)
        low_total += lax.dot_general(low_rows, at_low, NT_DIMS, preferred_element_type=F32)
    found = (high_total * 64.0 + low_total).astype(jnp.int32)
    inverse_ref[...] = jnp.clip(found, 0, perm_ref.shape[1] - 1)


def kernel(
    count,
    groups,
    q_hbm,
    k_hbm,
    v_hbm,
    g_hbm,
    perm_hbm,
    lists_hbm,
    bias_hbm,
    inverse_hbm,
    hot_hbm,
    o_ref,
    dq_ref,
    dk_ref,
    dv_ref,
    bias_out_ref,
    q_in,
    k_in,
    v_in,
    g_in,
    perm,
    lists,
    bias,
    inverse,
    hot,
    send_whole,
    land_whole,
    send_half,
    land_half,
    wide,
    rows_0,
    rows_1,
    rows_2,
    rows_3,
    key_query,
    key_t,
    query_t,
    query_low,
    value,
    value_t,
    grad_t,
    grad_low,
    scores,
    grads,
    probs,
    run_tile,
    run_row,
    bias_pairs,
    bias_own,
    bias_groups,
    bias_sum,
    bias_heads,
    local_sem,
    send_sem,
    recv_sem,
):
    me = lax.axis_index("seq")
    group = lax.axis_index("dp")
    tiles = key_query.shape[0]
    pairs = scores.shape[0]
    low = lanes_low()
    low_half = low[:64]
    rows_of = (rows_0, rows_1, rows_2, rows_3)
    run_key = grads
    low_grads = probs

    def peer(step):
        return lax.rem(me + step, count)

    def group_peer(step):
        return lax.rem(group + step, groups)

    def stage(number, source, target):
        return pltpu.make_async_copy(source, target, local_sem.at[number])

    staged = [
        stage(number, source, target)
        for number, (source, target) in enumerate(
            (
                (k_hbm, k_in),
                (q_hbm, q_in),
                (v_hbm, v_in),
                (g_hbm, g_in),
                (perm_hbm, perm),
                (lists_hbm, lists),
                (bias_hbm, bias),
                (inverse_hbm, inverse),
                (hot_hbm, hot),
            )
        )
    ]
    for copy in staged:
        copy.start()

    barrier = pltpu.get_barrier_semaphore()

    @pl.loop(1, count)
    def _(step):
        pl.semaphore_signal(barrier, inc=1, device_id=(group, peer(step)), device_id_type=MESH)

    @pl.loop(1, groups)
    def _(step):
        pl.semaphore_signal(barrier, inc=1, device_id=(group_peer(step), me), device_id_type=MESH)

    def remote(src, dst, which, other, other_group):
        return pltpu.make_async_remote_copy(
            src_ref=src,
            dst_ref=dst,
            send_sem=send_sem.at[which],
            recv_sem=recv_sem.at[which],
            device_id=(other_group, other),
            device_id_type=MESH,
        )

    KEY_QUERY, VALUE, GRAD, OUT, VALUE_GRAD, KEY_QUERY_GRAD = range(6)
    buffers = {
        KEY_QUERY: (send_whole.at[0], land_whole.at[0]),
        VALUE: (send_half.at[0], land_half.at[0]),
        GRAD: (send_half.at[1], land_half.at[1]),
        OUT: (send_half.at[2], land_half.at[2]),
        VALUE_GRAD: (send_half.at[3], land_half.at[3]),
        KEY_QUERY_GRAD: (send_whole.at[1], land_whole.at[1]),
    }

    def send_block(which, other):
        out, landing = buffers[which]
        remote(out.at[other], landing.at[me], which, other, group).start()

    def keep_own(which):
        out, landing = buffers[which]
        landing[me] = out[me]

    def all_blocks(which):
        out, landing = buffers[which]
        blocks = pl.ds(0, count - 1)
        return remote(out.at[blocks], landing.at[blocks], which, peer(1), group)

    def send_all(which):
        @pl.loop(1, count)
        def _(step):
            send_block(which, peer(step))

        keep_own(which)

    def columns_of(pair):
        return pl.ds(pl.multiple_of(pair * TILE, TILE), TILE)

    def rows_at(tile):
        return pl.ds(pl.multiple_of(tile * TILE, TILE), TILE)

    def pack(first_ref, second_ref, which):
        out, _ = buffers[which]

        def one(pair):
            columns = columns_of(pair)
            first, second = first_ref[0, :, columns], second_ref[0, :, columns]
            out[2 * pair] = jnp.where(low, first, rolled(second))
            out[2 * pair + 1] = jnp.where(low, rolled(first), second)

        unrolled(count // 2, ABREAST, one)

    def pack_half(source, which):
        out, _ = buffers[which]

        def one(pair):
            columns = columns_of(pair)
            top, bottom = source[0, pl.ds(0, 64), columns], source[0, pl.ds(64, 64), columns]
            out[2 * pair] = jnp.where(low_half, top, rolled(bottom))
            out[2 * pair + 1] = jnp.where(low_half, rolled(top), bottom)

        unrolled(count // 2, ABREAST, one)

    staged[0].wait()
    staged[1].wait()
    pack(k_in, q_in, KEY_QUERY)
    pl.semaphore_wait(barrier, count + groups - 2)
    send_all(KEY_QUERY)
    staged[2].wait()
    pack_half(v_in, VALUE)
    send_all(VALUE)
    staged[3].wait()
    pack_half(g_in, GRAD)
    send_all(GRAD)
    for copy in staged[4:]:
        copy.wait()

    def cluster(use):
        @pl.loop(0, tiles // ABREAST)
        def _(step):
            for u in range(ABREAST):
                base = (step * ABREAST + u) * TILE
                gather_rows(wide, rows_of[u], lambda r, base=base: perm[0, base + r])
            for u in range(ABREAST):
                use(step * ABREAST + u, rows_of[u][...])

    def widen(which):
        landing = buffers[which][1]

        def one(block):
            wide[rows_at(block), :] = landing[block].astype(F32)

        unrolled(count, ABREAST, one)

    def widen_half(which):
        landing = buffers[which][1]

        def one(block):
            both = landing[block].astype(F32)
            wide[rows_at(block), :] = jnp.concatenate([both, pltpu.roll(both, 64, 1)], axis=0)

        unrolled(count, ABREAST, one)

    empty = jnp.zeros((64, TILE), F32)

    def use_key_query(tile, block):
        key_query[tile] = block.astype(BF16)
        turned = block.T
        key_t[tile] = turned[:64].astype(BF16)
        query_t[tile] = jnp.concatenate([turned[64:] * 0.125, empty], axis=0).astype(BF16)
        query_low[tile] = pltpu.roll(jnp.where(low, 0.0, block * 0.125), 64, 1).astype(BF16)

    all_blocks(KEY_QUERY).wait_recv()
    widen(KEY_QUERY)
    cluster(use_key_query)

    def first_of(row, p):
        return (p == 0) | (lists[row, p] != lists[row, jnp.maximum(p - 1, 0)])

    def over_pairs(start, body):
        def chunk(step, carry):
            for u in range(UNROLL):
                carry = body(step * UNROLL + u, carry)
            return carry

        lax.fori_loop(0, pairs // UNROLL, chunk, start)

    none = jnp.zeros((8, TILE), F32)

    def score_pair(p, peak):
        t, j = lists[T_OF, p], lists[J_OF, p]
        product = jnp.dot(key_query[j], query_t[t], preferred_element_type=F32)
        score = product * LOG2E + bias[lists[C_OF, p], me] * LOG2E
        scores[p] = score
        before = jnp.where(first_of(T_OF, p), -jnp.inf, peak)
        peak = jnp.maximum(before, jnp.max(folded(score), axis=0))
        run_row[p] = peak
        return peak

    over_pairs(none, score_pair)
    run_row[...] = jnp.broadcast_to(jnp.max(run_row[...], axis=1, keepdims=True), run_row.shape)

    def power_pair(p, total):
        end = lists[T_LAST, lists[T_OF, p]]
        power = jnp.exp2(folded(scores[p]) - run_row[end][None])
        scores[p] = power.reshape(TILE, TILE)
        total = jnp.where(first_of(T_OF, p), 0.0, total) + jnp.sum(power, axis=0)
        bias_pairs[p] = total
        return total

    over_pairs(none, power_pair)
    bias_pairs[...] = jnp.broadcast_to(
        1.0 / jnp.sum(bias_pairs[...], axis=1, keepdims=True), bias_pairs.shape
    )

    def prob_pair(p, carry):
        end = lists[T_LAST, lists[T_OF, p]]
        prob = (folded(scores[p]) * bias_pairs[end][None]).reshape(TILE, TILE)
        scores[p] = prob
        probs[p] = prob.astype(BF16)
        return carry

    over_pairs(jnp.int32(0), prob_pair)

    def by_query_tile(left, right):
        def body(p, total):
            part = jnp.dot(left[lists[J_OF, p]], right[p], preferred_element_type=F32)
            total = jnp.where(first_of(T_OF, p), 0.0, total) + part
            run_tile[p] = total
            return total

        over_pairs(empty, body)

    def by_key_tile(left, right):
        def body(q, total):
            part = jnp.dot(
                left[lists[P_OF, q]], right[lists[TQ_OF, q]], preferred_element_type=F32
            )
            total = jnp.where(first_of(JQ_OF, q), 0.0, total) + part
            run_key[q] = total
            return total

        over_pairs(jnp.zeros((TILE, TILE), F32), body)

    def send_wide(which, half):
        out, _ = buffers[which]

        @pl.loop(0, count // ABREAST)
        def _(turn):
            for u in range(ABREAST):
                other = peer(turn * ABREAST + u + 1)
                gather_rows(
                    wide,
                    rows_of[u],
                    lambda r, other=other: inverse[2 * other + r // 64, r % 64],
                )
            for u in range(ABREAST):
                other = peer(turn * ABREAST + u + 1)
                block = rows_of[u][...]
                if half:
                    block = jnp.where(low_half, block[:64], pltpu.roll(block[64:], 64, 1))
                out[other] = block.astype(BF16)
            for u in range(ABREAST):
                step = turn * ABREAST + u + 1
                if u < ABREAST - 1:
                    send_block(which, peer(step))
                else:

                    @pl.when(step < count)
                    def _():
                        send_block(which, peer(step))

        keep_own(which)

    def use_value(tile, block):
        value[tile] = block.astype(BF16)
        value_t[tile] = block.T[:64].astype(BF16)

    all_blocks(VALUE).wait_recv()
    widen_half(VALUE)
    cluster(use_value)
    by_query_tile(value_t, probs)

    def turn_out(tile):
        of_query = run_tile[lists[T_LAST, tile]]
        wide[rows_at(tile), :] = jnp.concatenate([of_query, empty], axis=0).T

    unrolled(tiles, ABREAST, turn_out)
    send_wide(OUT, True)

    def use_grad(tile, block):
        grad_low[tile] = jnp.where(low, block, 0.0).astype(BF16)
        grad_t[tile] = jnp.concatenate([block.T[:64], empty], axis=0).astype(BF16)

    all_blocks(GRAD).wait_recv()
    widen_half(GRAD)
    cluster(use_grad)
    by_key_tile(probs, grad_low)

    def place_value_grad(tile):
        wide[rows_at(tile), :] = run_key[lists[J_LAST, tile]]

    unrolled(tiles, ABREAST, place_value_grad)
    send_wide(VALUE_GRAD, True)

    def prob_grad_pair(p, dots):
        t, j = lists[T_OF, p], lists[J_OF, p]
        product = jnp.dot(value[j], grad_t[t], preferred_element_type=F32)
        grads[p] = product
        dots = jnp.where(first_of(T_OF, p), 0.0, dots) + jnp.sum(
            folded(scores[p]) * folded(product), axis=0
        )
        run_row[p] = dots
        return dots

    over_pairs(none, prob_grad_pair)
    run_row[...] = jnp.broadcast_to(jnp.sum(run_row[...], axis=1, keepdims=True), run_row.shape)

    def score_grad_pair(p, carry):
        end = lists[T_LAST, lists[T_OF, p]]
        grad = folded(scores[p]) * (folded(grads[p]) - run_row[end][None])
        bias_pairs[p] = jnp.sum(grad, axis=0)
        low_grads[p] = grad.reshape(TILE, TILE).astype(BF16)
        return carry

    over_pairs(jnp.int32(0), score_grad_pair)
    by_query_tile(key_t, low_grads)
    by_key_tile(low_grads, query_low)

    def place_key_query_grad(tile):
        of_query = run_tile[lists[T_LAST, tile]] * 0.125
        of_key = run_key[lists[J_LAST, tile]]
        wide[rows_at(tile), :] = jnp.concatenate([empty, of_query], axis=0).T + of_key

    unrolled(tiles, ABREAST, place_key_query_grad)

    left = jnp.sum(bias_pairs[...], axis=1)
    class_sums = jnp.zeros((hot.shape[0], TILE), F32)
    hot_low = hot[...].astype(BF16)
    for _ in range(3):
        part = left.astype(BF16)
        class_sums += jnp.dot(hot_low, part, preferred_element_type=F32)
        left = left - part.astype(F32)
    own_column = iota(bias_own.shape, 1) == me
    bias_own[...] = jnp.where(own_column, jnp.sum(class_sums, axis=1, keepdims=True), 0.0)

    @pl.loop(1, groups)
    def _(step):
        remote(bias_own, bias_groups.at[group], 6, me, group_peer(step)).start()

    bias_groups[group] = bias_own[...]
    send_wide(KEY_QUERY_GRAD, False)

    own_groups = pl.ds(0, groups - 1)
    group_copies = remote(
        bias_groups.at[own_groups], bias_groups.at[own_groups], 6, me, group_peer(1)
    )
    group_copies.wait_recv()
    bias_sum[...] = jnp.sum(bias_groups[...], axis=0)

    @pl.loop(1, count)
    def _(step):
        remote(bias_sum, bias_heads.at[me], 7, peer(step), group).start()

    bias_heads[me] = bias_sum[...]

    def unpack_half(which, target):
        landing = buffers[which][1]

        def one(pair):
            even, odd = landing[2 * pair], landing[2 * pair + 1]
            target[pl.ds(0, 64), columns_of(pair)] = jnp.where(low_half, even, rolled(odd))
            target[pl.ds(64, 64), columns_of(pair)] = jnp.where(low_half, rolled(even), odd)

        unrolled(count // 2, ABREAST, one)

    def unpack(which, first_ref, second_ref):
        landing = buffers[which][1]

        def one(pair):
            even, odd = landing[2 * pair], landing[2 * pair + 1]
            first_ref[:, columns_of(pair)] = jnp.where(low, even, rolled(odd))
            second_ref[:, columns_of(pair)] = jnp.where(low, rolled(even), odd)

        unrolled(count // 2, ABREAST, one)

    all_blocks(OUT).wait_recv()
    unpack_half(OUT, o_ref)
    all_blocks(VALUE_GRAD).wait_recv()
    unpack_half(VALUE_GRAD, dv_ref)
    own_heads = pl.ds(0, count - 1)
    head_copies = remote(bias_heads.at[own_heads], bias_heads.at[own_heads], 7, peer(1), group)
    head_copies.wait_recv()
    bias_out_ref[...] = jnp.sum(bias_heads[...], axis=0)[:, : bias_out_ref.shape[1]]
    for which in (KEY_QUERY, VALUE, GRAD, OUT, VALUE_GRAD):
        all_blocks(which).wait_send()
    group_copies.wait_send()
    head_copies.wait_send()
    all_blocks(KEY_QUERY_GRAD).wait_recv()
    unpack(KEY_QUERY_GRAD, dk_ref, dq_ref)
    all_blocks(KEY_QUERY_GRAD).wait_send()


def plan(perm_ref, ids_ref, counts_ref, class_ref, list_ref, inverse_ref, hot_ref):
    write_lists(ids_ref, counts_ref, class_ref, list_ref, hot_ref)
    write_inverse(perm_ref, inverse_ref)


def write_out(*refs):
    sources, targets, sems = refs[:5], refs[5:10], refs[10]
    copies = []
    for number, (source, target) in enumerate(zip(sources, targets)):
        place = target if number == 4 else target.at[0]
        copies.append(pltpu.make_async_copy(source, place, sems.at[number]))
    for copy in copies:
        copy.start()
    for copy in copies:
        copy.wait()


def local(
    queries, keys, values, out_grad, cluster_perm, tile_ids, tile_counts, hop_class, hop_bias
):
    count, groups = lax.axis_size("seq"), lax.axis_size("dp")
    nodes = cluster_perm.shape[1]
    tiles = nodes // TILE
    columns = queries.shape[2]
    classes, heads = hop_bias.shape
    pairs = TILE
    i32 = jnp.int32
    any_space = pl.BlockSpec(memory_space=pl.ANY)
    vmem = pl.BlockSpec(memory_space=pltpu.VMEM)
    one_output = jax.ShapeDtypeStruct((TILE, columns), BF16)
    bias_output = jax.ShapeDtypeStruct((classes, heads), F32)
    tile_blocks = pltpu.VMEM((tiles, TILE, TILE), BF16)
    half_blocks = pltpu.VMEM((tiles, 64, TILE), BF16)

    lists, inverse, hot = pl.pallas_call(
        plan,
        out_shape=(
            jax.ShapeDtypeStruct((8, TILE), i32),
            jax.ShapeDtypeStruct((64, 64), i32),
            jax.ShapeDtypeStruct((classes, TILE), F32),
        ),
        in_specs=[vmem] * 4,
        out_specs=(vmem,) * 3,
        compiler_params=pltpu.CompilerParams(vmem_limit_bytes=4 << 20),
        name="plan",
    )(
        cluster_perm,
        jnp.swapaxes(tile_ids, 1, 2),
        tile_counts,
        jnp.swapaxes(hop_class, 1, 2),
    )

    results = pl.pallas_call(
        functools.partial(kernel, count, groups),
        out_shape=(one_output,) * 4 + (bias_output,),
        in_specs=[any_space] * 9,
        out_specs=(vmem,) * 5,
        scratch_shapes=[pltpu.VMEM((1, TILE, columns), BF16)] * 4
        + [
            pltpu.SMEM((1, nodes), i32),
            pltpu.SMEM((8, TILE), i32),
            pltpu.SMEM(hop_bias.shape, F32),
            pltpu.SMEM((64, 64), i32),
            pltpu.VMEM((classes, TILE), F32),
            pltpu.VMEM((2, count, TILE, TILE), BF16),
            pltpu.VMEM((2, count, TILE, TILE), BF16),
            pltpu.VMEM((4, count, 64, TILE), BF16),
            pltpu.VMEM((4, count, 64, TILE), BF16),
            pltpu.VMEM((nodes, TILE), F32),
        ]
        + [pltpu.VMEM((TILE, TILE), F32)] * 4
        + [
            tile_blocks,
            half_blocks,
            tile_blocks,
            tile_blocks,
            tile_blocks,
            half_blocks,
            tile_blocks,
            tile_blocks,
            pltpu.VMEM((pairs, TILE, TILE), F32),
            pltpu.VMEM((pairs, TILE, TILE), F32),
            pltpu.VMEM((pairs, TILE, TILE), BF16),
            pltpu.VMEM((pairs, 64, TILE), F32),
            pltpu.VMEM((pairs, 8, TILE), F32),
            pltpu.VMEM((pairs, 8, TILE), F32),
            pltpu.VMEM((classes, TILE), F32),
            pltpu.VMEM((groups, classes, TILE), F32),
            pltpu.VMEM((classes, TILE), F32),
            pltpu.VMEM((count, classes, TILE), F32),
            pltpu.SemaphoreType.DMA((9,)),
            pltpu.SemaphoreType.DMA((8,)),
            pltpu.SemaphoreType.DMA((8,)),
        ],
        compiler_params=pltpu.CompilerParams(
            collective_id=0, has_side_effects=True, vmem_limit_bytes=103 << 19
        ),
        name="graph_attention",
    )(
        queries,
        keys,
        values,
        out_grad,
        cluster_perm,
        lists,
        hop_bias,
        inverse,
        hot,
    )

    whole_output = jax.ShapeDtypeStruct((1, TILE, columns), BF16)
    return pl.pallas_call(
        write_out,
        out_shape=(whole_output,) * 4 + (bias_output,),
        in_specs=[vmem] * 5,
        out_specs=(any_space,) * 5,
        scratch_shapes=[pltpu.SemaphoreType.DMA((5,))],
        compiler_params=pltpu.CompilerParams(vmem_limit_bytes=1 << 20),
        name="write_out",
    )(*results)


def solution(mesh):
    wide = P("dp", "seq", None)
    return jax.shard_map(
        local,
        mesh=mesh,
        in_specs=(
            wide,
            wide,
            wide,
            wide,
            P("dp", None),
            P("dp", None, None),
            P("dp", None),
            P("dp", None, None),
            P(),
        ),
        out_specs=(wide, wide, wide, wide, P()),
        check_vma=False,
    )
```
